128 devices in a mesh: dp: 4 (over x), seq: 16 (over z, y), tensor: 2 (over core).
Axes of the slice: x: 4, y: 4, z: 4, core: 2. Of those that a mesh axis runs over, the one named last changes fastest.
Arguments:
- hidden_in: bfloat16 [16384, 2048], P(('dp', 'seq', 'tensor')), parts along dimension 0, may hold values from -36 to 36
- attn_gain: float32 [2048], replicated, may hold values from 0.25 to 1.75
- query_weight: bfloat16 [2048, 4096], P('seq', 'tensor'), may hold values from -32 to 32
- key_weight: bfloat16 [2048, 1024], P('seq', 'tensor'), may hold values from -0.125 to 0.125
- value_weight: bfloat16 [2048, 1024], P('seq', 'tensor'), may hold values from -0.125 to 0.125
- out_weight: bfloat16 [4096, 2048], P('tensor', 'seq'), may hold values from -0.09375 to 0.09375
- mlp_gain: float32 [2048], replicated, may hold values from 0.25 to 1.75
- gate_weight: bfloat16 [2048, 7168], P('seq', 'tensor'), may hold values from -0.125 to 0.125
- up_weight: bfloat16 [2048, 7168], P('seq', 'tensor'), may hold values from -0.125 to 0.125
- down_weight: bfloat16 [7168, 2048], P('tensor', 'seq'), may hold values from -0.0625 to 0.0625
- segment_ids: int32 [16384], P(('dp', 'seq', 'tensor')), parts along dimension 0, may hold values from 0 to 15, never falling along the last dimension, each value on 1 to 2048 neighbouring positions
- modality: int32 [16384], P(('dp', 'seq', 'tensor')), parts along dimension 0, may hold values 0 or 1
Outputs:
- result: bfloat16 [16384, 2048], P(('dp', 'seq', 'tensor')), parts along dimension 0
The draws below stay inside these ranges and needn't reach their ends.
There are 4 independent parts, one for each index of `dp`. The reference program is written for one: setup_inputs(seed, part) draws one part's arguments, and reference() takes and returns one part's arrays. A program takes and returns all parts, laid end to end along the dimension named above; an argument that names none is the same for every part. Nothing has to cross between parts.
Inputs may be any that keep to these rules, and one draw needn't show every extreme that they name: `segment_ids`: never falling along the sequence; each document holds 1 to 2048 tokens, and one holds exactly that many.
All inputs are finite; a program needn't handle non-finite values. No bound on the sum of `modality` on one device may be relied on, other than what follows from the above.
Results may differ from the reference program's by a relative error of at most 0.015.
Values may be sent and summed in bfloat16 or wider, within the bound.
No kernel may reach another device: no remote copies, remote signals or barrier semaphores. Data moves between devices by JAX's collectives and lax.ppermute only.
A program may use at most 128 MiB of HBM per device.

```python
import math
import jax
import jax.numpy as jnp
import numpy as np
from jax import lax

D = 2048
HEADS = 32
KV_HEADS = 8
HEAD_DIM = 128
FF = 7168
SEQ_LEN = 4096
SEGMENTS = 16


def draw_hidden_in(key, part):
    key = jax.random.fold_in(key, 11)
    row_key, column_key, value_key = jax.random.split(key, 3)
    row_scale = jnp.exp(jax.random.uniform(row_key, (SEQ_LEN, 1), jnp.float32, math.log(0.3), math.log(3.0)))
    column_scale = jnp.exp(jax.random.uniform(column_key, (1, D), jnp.float32, math.log(0.3), math.log(3.0)))
    values = jax.random.truncated_normal(value_key, -4.0, 4.0, (SEQ_LEN, D), jnp.float32)
    return (values * row_scale * column_scale).astype(jnp.bfloat16)


def draw_query_weight(key, part):
    key = jax.random.fold_in(key, 23)
    value_key = jax.random.fold_in(key, 0)
    values = jax.random.truncated_normal(value_key, -4.0, 4.0, (D, HEADS * HEAD_DIM), jnp.float32) * D ** (-0.5)
    return values.astype(jnp.bfloat16)


def with_ends(values, key, smallest, high):
    spot = [jax.random.randint(jax.random.fold_in(key, axis), (), 0, length) for axis, length in enumerate(values.shape)]
    widest = values.shape.index(max(values.shape))
    next_to = spot[:widest] + [(spot[widest] + 1) % values.shape[widest]] + spot[widest + 1:]
    return values.at[tuple(spot)].set(smallest).at[tuple(next_to)].set(high)


def block_levels(own_key, extent, cuts, smallest, top_value):
    loudness = 1.0
    for position, blocks in cuts:
        steps = jax.random.uniform(jax.random.fold_in(jax.random.fold_in(own_key, 6), position), (blocks,), jnp.float32, smallest / len(cuts), top_value / len(cuts))
        loudness = loudness * jnp.repeat(jnp.exp(steps), extent[position] // blocks).reshape((-1,) + (1,) * (len(extent) - 1 - position))
    return loudness


def length_profile(amount, total, most, slope):
    loads = [(1 << 20) // math.isqrt(standing ** slope) + 1 for standing in range(2, amount + 1)]
    surplus, given = total - most - (amount - 1), [1] * (amount - 1)
    while surplus > 0:
        free = [i for i in range(amount - 1) if given[i] < most]
        mass, remaining = sum([loads[i] for i in free]), surplus
        for i in free:
            addition = min(most - given[i], max(1, remaining * loads[i] // mass), surplus)
            given[i] = given[i] + addition
            surplus = surplus - addition
    return np.array([most] + given)


def uneven_parts(stream_key, count, total, most, slope):
    if count == 2:
        one = jax.random.randint(stream_key, (), max(1, total - most), min(most, total - 1) + 1)
        return jnp.stack([one, total - one])
    tallies = jnp.asarray(length_profile(count, total, most, slope), jnp.int32)
    twos = (count - 1) // 2
    giver, taker = tallies[1:1 + 2 * twos:2], tallies[2:2 + 2 * twos:2]
    room = jnp.minimum(giver - 1, most - taker)
    moved = jax.random.randint(jax.random.fold_in(stream_key, 1), (twos,), 0, 1 << 20) % (room + 1)
    tallies = tallies.at[1:1 + 2 * twos:2].set(giver - moved).at[2:2 + 2 * twos:2].set(taker + moved)
    return tallies[jax.random.permutation(jax.random.fold_in(stream_key, 2), count)]


def bell_draw(own_key, shape, scale, most, pieces=(), kind=jnp.bfloat16):
    values = jax.random.normal(own_key, shape, jnp.float32) * scale
    if len(pieces) > 0:
        values = block_levels(own_key, shape, pieces, -0.22, 0.18) * values
    return jnp.clip(values, min=-most, max=most).astype(kind)


def setup_inputs(seed: int = 0, part: int = 0) -> dict:
    splits = jax.random.split(jax.random.key(seed), 13)
    own_keys = jax.random.split(jax.random.fold_in(splits[12], part), 13)
    hidden_in = draw_hidden_in(jax.random.fold_in(jax.random.fold_in(splits[12], part), 71), part)
    attn_gain = jnp.clip(1.0 + 0.15 * jax.random.normal(splits[1], (D,), jnp.float32), 0.25, 1.75)
    query_weight = draw_query_weight(jax.random.fold_in(splits[12], 71), part)
    key_weight = bell_draw(splits[3], (D, KV_HEADS * HEAD_DIM), D ** -0.5, 0.125, ((0, 16), (1, 2)))
    value_weight = bell_draw(splits[4], (D, KV_HEADS * HEAD_DIM), D ** -0.5, 0.125, ((0, 16), (1, 2)))
    out_weight = bell_draw(splits[5], (HEADS * HEAD_DIM, D), (HEADS * HEAD_DIM) ** -0.5, 0.09375, ((0, 2), (1, 16)))
    mlp_gain = jnp.clip(1.0 + 0.15 * jax.random.normal(splits[6], (D,), jnp.float32), 0.25, 1.75)
    gate_weight = bell_draw(splits[7], (D, FF), D ** -0.5, 0.125, ((0, 16), (1, 2)))
    up_weight = bell_draw(splits[8], (D, FF), D ** -0.5, 0.125, ((0, 16), (1, 2)))
    down_weight = bell_draw(splits[9], (FF, D), FF ** -0.5, 0.0625, ((0, 2), (1, 16)))
    segment_ids = jnp.searchsorted(jnp.cumsum(uneven_parts(own_keys[10], SEGMENTS, SEQ_LEN, SEQ_LEN // 2, 2)), jnp.arange(SEQ_LEN), side="right").astype(jnp.int32)
    modality = with_ends((jax.random.randint(own_keys[11], (SEQ_LEN,), 0, 2) < 1).astype(jnp.int32), jax.random.fold_in(own_keys[11], 1), 0, 1)
    return dict(hidden_in=hidden_in, attn_gain=attn_gain, query_weight=query_weight, key_weight=key_weight, value_weight=value_weight, out_weight=out_weight, mlp_gain=mlp_gain, gate_weight=gate_weight, up_weight=up_weight, down_weight=down_weight, segment_ids=segment_ids, modality=modality)


EPSILON = 1e-05
THETA = 500000.0

def rms_normed(values, gain_vec):
    widened = values.astype(jnp.float32)
    mean_square = lax.optimization_barrier(jnp.mean(widened * widened, axis=-1, keepdims=True))
    return (widened * lax.rsqrt(mean_square + EPSILON) * gain_vec).astype(jnp.bfloat16)

def rotary(values, positions):
    half_dim = values.shape[-1] // 2
    inverse_freq = THETA ** (-2.0 * jnp.arange(half_dim, dtype=jnp.float32) / values.shape[-1])
    angles = positions.astype(jnp.float32)[:, None] * inverse_freq[None, :]
    cosine = jnp.cos(angles)[:, None, :]
    sine_part = jnp.sin(angles)[:, None, :]
    first_half = values[..., :half_dim]
    second_half = values[..., half_dim:]
    return jnp.concatenate([first_half * cosine - second_half * sine_part, second_half * cosine + first_half * sine_part], axis=-1)

def visible(query_seg, query_mod, query_pos, key_seg, key_mod, key_pos):
    same_doc = query_seg[:, None] == key_seg[None, :]
    earlier = key_pos[None, :] <= query_pos[:, None]
    both_video = (query_mod[:, None] == 1) & (key_mod[None, :] == 1)
    return same_doc & (earlier | both_video)

def attend_head(query_head, key_head, value_head, segment_ids, modality):
    length = query_head.shape[0]
    block_rows = min(512, length)
    positions = jnp.arange(length, dtype=jnp.int32)
    scale_factor = query_head.shape[-1] ** (-0.5)

    def one_block(block_index):
        row_start = block_index * block_rows
        query_block = lax.dynamic_slice_in_dim(query_head, row_start, block_rows, 0)
        allowed = visible(lax.dynamic_slice_in_dim(segment_ids, row_start, block_rows, 0), lax.dynamic_slice_in_dim(modality, row_start, block_rows, 0), lax.dynamic_slice_in_dim(positions, row_start, block_rows, 0), segment_ids, modality, positions)
        scores = jnp.dot(query_block, key_head.T, preferred_element_type=jnp.float32) * scale_factor
        scores = jnp.where(allowed, scores, -1e+30)
        row_max = lax.optimization_barrier(jnp.max(scores, axis=-1, keepdims=True))
        exp_terms = jnp.where(allowed, jnp.exp(scores - row_max), 0.0)
        denominator = lax.optimization_barrier(jnp.sum(exp_terms, axis=-1, keepdims=True))
        mixed = jnp.dot(exp_terms.astype(jnp.bfloat16), value_head, preferred_element_type=jnp.float32)
        return (mixed / denominator).astype(jnp.bfloat16)
    blocks = lax.map(one_block, jnp.arange(length // block_rows, dtype=jnp.int32))
    return blocks.reshape(length, query_head.shape[-1])

def reference(hidden_in, attn_gain, query_weight, key_weight, value_weight, out_weight, mlp_gain, gate_weight, up_weight, down_weight, segment_ids, modality):
    length = hidden_in.shape[0]
    positions = jnp.arange(length, dtype=jnp.int32)
    normed = rms_normed(hidden_in, attn_gain)
    queries = jnp.dot(normed, query_weight, preferred_element_type=jnp.float32).reshape(length, HEADS, HEAD_DIM)
    queries = rotary(queries, positions).astype(jnp.bfloat16)
    key_rows = jnp.dot(normed, key_weight, preferred_element_type=jnp.float32).reshape(length, KV_HEADS, HEAD_DIM)
    key_rows = rotary(key_rows, positions).astype(jnp.bfloat16)
    value_rows = jnp.dot(normed, value_weight, preferred_element_type=jnp.float32).astype(jnp.bfloat16)
    value_rows = value_rows.reshape(length, KV_HEADS, HEAD_DIM)
    group_size = HEADS // KV_HEADS
    head_major = jnp.transpose(queries, (1, 0, 2))
    key_major = jnp.repeat(jnp.transpose(key_rows, (1, 0, 2)), group_size, axis=0)
    value_major = jnp.repeat(jnp.transpose(value_rows, (1, 0, 2)), group_size, axis=0)

    def per_head(operands):
        return attend_head(operands[0], operands[1], operands[2], segment_ids, modality)
    attended = lax.map(per_head, (head_major, key_major, value_major))
    attended = jnp.transpose(attended, (1, 0, 2)).reshape(length, HEADS * HEAD_DIM)
    projected = jnp.dot(attended, out_weight, preferred_element_type=jnp.float32)
    residual = (hidden_in.astype(jnp.float32) + projected).astype(jnp.bfloat16)
    normed_two = rms_normed(residual, mlp_gain)
    gate_proj = jnp.dot(normed_two, gate_weight, preferred_element_type=jnp.float32)
    up_proj = jnp.dot(normed_two, up_weight, preferred_element_type=jnp.float32)
    inner_act = (jax.nn.silu(gate_proj) * up_proj).astype(jnp.bfloat16)
    down_part = jnp.dot(inner_act, down_weight, preferred_element_type=jnp.float32)
    return (residual.astype(jnp.float32) + down_part).astype(jnp.bfloat16)
```

```python
import functools

import jax
import jax.numpy as jnp
from jax import lax
from jax.experimental import pallas as pl
from jax.experimental.pallas import tpu as pltpu
from jax.sharding import PartitionSpec as P

HEADS = 32
KV_HEADS = 8
HEAD_DIM = 128
EPSILON = 1e-05
THETA = 500000.0
SIDE = 4
BF16 = jnp.bfloat16
F32 = jnp.float32
SMEM = pl.BlockSpec(memory_space=pltpu.SMEM)
STEPS = (0, -1, 1, 2)


def x_shift(value, step):
    return lax.ppermute(value, "dp", [(i, (i + step) % SIDE) for i in range(SIDE)])


def y_shift(value, step):
    return lax.ppermute(value, "y", [(i, (i + step) % SIDE) for i in range(SIDE)])


def z_shift(value, step):
    return lax.ppermute(value, "z", [(i, (i + step) % SIDE) for i in range(SIDE)])


def plane_shift(value, axis):
    moved = lax.ppermute(
        value,
        ("dp", axis),
        [(x * SIDE + (i + x) % SIDE, x * SIDE + i) for x in range(1, SIDE) for i in range(SIDE)],
    )
    return jnp.where(lax.axis_index("dp") == 0, value, moved)


def swap_cores(value):
    return lax.ppermute(value, "tensor", [(0, 1), (1, 0)])


def ring_gather(value, shift):
    return [value if step == 0 else shift(value, -step) for step in STEPS]


def in_order(values, *earlier):
    kept = lax.optimization_barrier((values, earlier))
    return kept[0]


def place_tokens(mine, theirs, whole):
    rows = mine[0].shape[0]
    for which, pieces in enumerate((mine, theirs)):
        for place in range(SIDE):
            start = (2 * place + which) * rows
            for piece in pieces[place : None if place == 3 else place + 1]:
                whole[start : start + piece.shape[0], :] = piece[...]
                start += piece.shape[0]


def plane_blocks(pieces, rows):
    for piece in pieces:
        for start in range(0, piece.shape[0], rows):
            yield piece, start


def cut_kernel(places, query, key, value, info, gate, up, down, *refs):
    parts, packed = refs[:-1], refs[-1]
    rows = query.shape[0]
    for turn in range(SIDE):
        place = places[turn]
        part = parts[turn]
        wide, narrow = pl.multiple_of(place * 512, 512), pl.multiple_of(place * 128, 128)
        part[:rows, :512] = query[:, pl.ds(wide, 512)]
        part[:rows, 512:640] = key[:, pl.ds(narrow, 128)]
        part[:rows, 640:] = value[:, pl.ds(narrow, 128)]
        part[rows:, :] = info[...]
    units = gate.shape[1]
    for block in range(units // 128):
        start = block * 128
        packed[start : start + 128, :] = gate[:, start : start + 128]
        packed[units + start : units + start + 128, :] = up[:, start : start + 128]
    packed[2 * units :, :] = down[...]


def rms_normed(values, gain_vec):
    widened = values.astype(F32)
    mean_square = jnp.mean(widened * widened, axis=-1, keepdims=True)
    return (widened * lax.rsqrt(mean_square + EPSILON) * gain_vec).astype(BF16)


def qkv_kernel(offsets, *refs):
    mine, theirs, weights = refs[0:5], refs[5:10], refs[10:17]
    cosine, sine, query_out, kv_out, tokens, table = refs[17:]
    place_tokens(mine, theirs, tokens)
    depth = 128
    for slot, (source, start) in enumerate(plane_blocks(weights, weights[3].shape[0])):
        row = pl.multiple_of(offsets[slot], depth)
        table[pl.ds(row, depth), :] = source[start : start + depth, :]
    cos_all, sin_all = cosine[...], sine[...]

    def rotated(part):
        return part * cos_all + pltpu.roll(part, HEAD_DIM // 2, 1) * sin_all

    for block in range(3):
        sums = jnp.dot(
            tokens[...], table[:, block * 256 : block * 256 + 256], preferred_element_type=F32
        )
        first, second = sums[:, :HEAD_DIM], sums[:, HEAD_DIM:]
        if block < 2:
            query_out[:, block * 256 : block * 256 + HEAD_DIM] = rotated(first).astype(BF16)
            query_out[:, block * 256 + HEAD_DIM : block * 256 + 256] = rotated(second).astype(BF16)
        else:
            kv_out[:, :HEAD_DIM] = rotated(first).astype(BF16)
            kv_out[:, HEAD_DIM:] = second.astype(BF16)


def attend_kernel(block_rows, z_place, kinds, query, query_info, key_info, *refs):
    kv_pieces, table = refs[0:4], refs[4]
    own_out, other_out, kv_all, scores, top, total, mixed = refs[5:]
    group = HEADS // KV_HEADS
    scale = HEAD_DIM**-0.5 * 1.4426950408889634
    for slot in range(16):
        start = slot % SIDE * block_rows
        kv_all[slot] = kv_pieces[slot // SIDE][start : start + block_rows, :]
    top[...] = jnp.full(top.shape, -1e30, F32)
    total[...] = jnp.zeros_like(total)
    mixed[...] = jnp.zeros_like(mixed)

    def score_of(head, key):
        return lax.dot_general(
            query[:, head * HEAD_DIM : (head + 1) * HEAD_DIM],
            key,
            (((1,), (1,)), ((), ())),
            preferred_element_type=F32,
        )

    def keep(slot, head, score):
        scores[slot, head] = score
        top[head] = jnp.maximum(
            top[head], jnp.maximum(score[:, :HEAD_DIM], score[:, HEAD_DIM:])
        )

    def first_pass(slot, carry):
        kind = kinds[z_place * 16 + slot]

        @pl.when(kind == 1)
        def _():
            key = kv_all[slot, :, :HEAD_DIM]
            for head in range(group):
                keep(slot, head, score_of(head, key))

        @pl.when(kind == 2)
        def _():
            key = kv_all[slot, :, :HEAD_DIM]
            key_seg = key_info[pl.ds(slot, 1), :]
            key_video = key_info[pl.ds(16 + slot, 1), :]
            key_pos = key_info[pl.ds(32 + slot, 1), :]
            same = query_info[:, 0:1] == key_seg
            video = query_info[:, 1:2] == key_video
            earlier = key_pos <= query_info[:, 2:3]
            allowed = video | (same & earlier)
            for head in range(group):
                keep(slot, head, jnp.where(allowed, score_of(head, key), -1e30))

        return carry

    lax.fori_loop(0, 16, first_pass, 0)
    for head in range(group):
        top[head] = jnp.broadcast_to(
            jnp.max(top[head], axis=-1, keepdims=True), top.shape[1:]
        )

    def second_pass(slot, carry):
        @pl.when(kinds[z_place * 16 + slot] > 0)
        def _():
            value = kv_all[slot, :, HEAD_DIM:]
            for head in range(group):
                high = top[head]
                left = jnp.exp2((scores[slot, head, :, :HEAD_DIM] - high) * scale)
                right = jnp.exp2((scores[slot, head, :, HEAD_DIM:] - high) * scale)
                total[head] = total[head] + (left + right)
                terms = jnp.concatenate([left.astype(BF16), right.astype(BF16)], axis=1)
                mixed[head] = mixed[head] + jnp.dot(terms, value, preferred_element_type=F32)

        return carry

    lax.fori_loop(0, 16, second_pass, 0)
    attended = jnp.concatenate(
        [
            (mixed[head] / jnp.sum(total[head], axis=-1, keepdims=True)).astype(BF16)
            for head in range(group)
        ],
        axis=1,
    )
    half = block_rows // 2
    for start in range(0, table.shape[1], 512):
        part = jnp.dot(
            attended, table[:, start : start + 512], preferred_element_type=F32
        ).astype(BF16)
        own_out[:, start : start + 512] = part[:half]
        other_out[:, start : start + 512] = part[half:]


def table_kernel(offsets, *refs):
    pieces, table = refs[:-1], refs[-1]
    depth = table.shape[0]
    for slot, (source, start) in enumerate(plane_blocks(pieces, depth)):
        column = pl.multiple_of(offsets[slot], 128)
        table[:, pl.ds(column, 128)] = source[start : start + depth, :]


def lift_kernel(offsets, *refs):
    mine, theirs = refs[0:4], refs[4:8]
    gate, up, inner, tokens = refs[8:]

    @pl.when(pl.program_id(0) == 0)
    def _():
        rows = mine[0].shape[0]
        for block in range(16):
            column = pl.multiple_of(offsets[block], 128)
            for place, pair in enumerate(zip(mine, theirs)):
                for which, piece in enumerate(pair):
                    start = (2 * place + which) * rows
                    tokens[start : start + rows, block * 128 : block * 128 + 128] = piece[
                        :, pl.ds(column, 128)
                    ]

    pair = jnp.concatenate([gate[...].reshape(-1, 128), up[...].reshape(-1, 128)], axis=1)
    sums = jnp.dot(tokens[...], pair, preferred_element_type=F32)
    gated, lifted = sums[:, :128], sums[:, 128:]
    inner[0] = (gated / (1.0 + jnp.exp(-gated)) * lifted).astype(BF16)


def lower_kernel(offsets, inner, down, own_out, other_out):
    blocks, rows = inner.shape[0], inner.shape[1]
    step = pl.program_id(0)
    lhs = jnp.concatenate([inner[block] for block in range(blocks)], axis=1)
    rhs = jnp.concatenate([down[0], down[1]], axis=1)
    part = jnp.dot(lhs, rhs, preferred_element_type=F32).astype(BF16)
    part = part.reshape(SIDE, 2, rows // 8, 256)
    for out, which in ((own_out, 0), (other_out, 1)):
        flat = part[:, which].reshape(rows // 2, 256)
        for side in range(2):
            column = pl.multiple_of(offsets[2 * step + side], 128)
            out[:, pl.ds(column, 128)] = flat[:, side * 128 : side * 128 + 128]


def whole_block(array):
    return pl.BlockSpec(array.shape, lambda *step: (0,) * array.ndim)


def call(kernel, out_shape, *operands, scalars=(), specs=None, scratch=(), cost=(1, 1, 0), name):
    specs = [whole_block(array) for array in operands] if specs is None else specs
    return pl.pallas_call(
        kernel,
        out_shape=out_shape,
        grid=(1,),
        in_specs=[SMEM] * len(scalars) + specs,
        out_specs=jax.tree.map(whole_block, out_shape),
        scratch_shapes=list(scratch),
        compiler_params=pltpu.CompilerParams(vmem_limit_bytes=48 << 20),
        cost_estimate=pl.CostEstimate(
            flops=cost[0], bytes_accessed=cost[1], transcendentals=cost[2]
        ),
        name=name,
    )(*scalars, *operands)


def per_device(
    hidden_in,
    attn_gain,
    query_weight,
    key_weight,
    value_weight,
    out_weight,
    mlp_gain,
    gate_weight,
    up_weight,
    down_weight,
    segment_ids,
    modality,
):
    x, z, y = lax.axis_index("dp"), lax.axis_index("z"), lax.axis_index("y")
    core = lax.axis_index("tensor")
    rows, width = hidden_in.shape
    block_rows = 2 * rows
    z_places = [(z + step) % SIDE for step in STEPS]
    y_places = [(y + step) % SIDE for step in STEPS]
    block_ids = jnp.stack([zz * SIDE + yy for yy in y_places for zz in z_places]).astype(jnp.int32)
    x_places = jnp.stack([(x + step) % SIDE for step in STEPS]).astype(jnp.int32)
    qkv_offsets = jnp.concatenate([block_ids[:12], jnp.take(block_ids[12:], x_places)]) * 128

    info = jnp.concatenate([segment_ids, modality]).astype(BF16).reshape(1, 2 * rows)
    info_rows = jnp.pad(info, ((0, 15), (0, 768 - 2 * rows)))

    hidden_units = gate_weight.shape[1] // SIDE
    blocks = hidden_units // 128
    places = jnp.stack([(z - step) % SIDE for step in STEPS] + [(y - x) % SIDE]).astype(jnp.int32)
    cuts = [
        jax.ShapeDtypeStruct(shape, BF16)
        for shape in [(rows + 16, 768)] * SIDE + [(3 * hidden_units, 128)]
    ]
    whole = [query_weight, key_weight, value_weight, info_rows]
    cuts = pl.pallas_call(
        cut_kernel,
        out_shape=cuts,
        grid_spec=pltpu.PrefetchScalarGridSpec(
            num_scalar_prefetch=1,
            grid=(1,),
            in_specs=[whole_block(array) for array in whole]
            + [pl.BlockSpec((128, hidden_units), lambda i, place: (0, place[SIDE]))] * 2
            + [pl.BlockSpec((hidden_units, 128), lambda i, place: (place[SIDE], 0))],
            out_specs=[whole_block(cut) for cut in cuts],
        ),
        compiler_params=pltpu.CompilerParams(vmem_limit_bytes=58 << 20),
        cost_estimate=pl.CostEstimate(flops=1, bytes_accessed=4 << 20, transcendentals=0),
        name="cut",
    )(places, *whole, gate_weight, up_weight, down_weight)

    def from_ring(parts):
        return [
            part if step == 0 else z_shift(part, -step) for part, step in zip(parts, STEPS)
        ]

    out_part = lax.dynamic_slice_in_dim(out_weight, (z - x) % SIDE * 512, 512, 0)
    out_all = lax.all_gather(plane_shift(out_part, "z"), ("dp", "y"), axis=0, tiled=True)
    out_places = [(z + plane) % SIDE * SIDE + yy for plane in range(SIDE) for yy in range(SIDE)]
    out_offsets = jnp.stack(out_places).astype(jnp.int32) * 128

    normed = rms_normed(hidden_in, attn_gain)
    qkv_ring = from_ring(cuts[:SIDE])
    near = [z_shift(normed, 1), z_shift(normed, -1)]
    mlp_part = plane_shift(cuts[-1], "y")
    qkv_ring, near, mlp_part = lax.optimization_barrier((qkv_ring, near, mlp_part))

    qkv_plane = jnp.concatenate(qkv_ring, axis=0)
    part_rows = qkv_ring[0].shape[0]
    quarter = y_shift(lax.dynamic_slice_in_dim(qkv_plane, x * part_rows, part_rows, 0), 2)
    qkv_near = [y_shift(qkv_plane, 1), y_shift(qkv_plane, -1)]
    qkv_pieces = [qkv_plane] + qkv_near + ring_gather(quarter, x_shift)
    info_far = y_shift(jnp.concatenate([part[rows : rows + 1, : 2 * rows] for part in qkv_ring]), 2)
    half = rows // 2
    far = [z_shift(near[1][:half], -1), z_shift(near[0][half:], 1)]
    mine = [normed] + near + far
    theirs = [swap_cores(piece) for piece in mine]
    mine, theirs, qkv_pieces = lax.optimization_barrier((mine, theirs, qkv_pieces))

    mlp_weights = lax.all_gather(mlp_part, ("dp", "z"), axis=0, tiled=False)
    mlp_places = [zz * SIDE + (y + plane) % SIDE for plane in range(SIDE) for zz in range(SIDE)]
    mlp_offsets = jnp.stack(mlp_places).astype(jnp.int32) * 128

    in_block = (jnp.arange(block_rows, dtype=jnp.int32) + core * rows) % block_rows
    block_pos = block_ids[:, None] * block_rows + in_block[None, :]
    half_dim = HEAD_DIM // 2
    inverse_freq = THETA ** (-2.0 * jnp.arange(half_dim, dtype=F32) / HEAD_DIM)
    angles = block_pos[:SIDE].reshape(-1).astype(F32)[:, None] * inverse_freq[None, :]
    cosine, sine = jnp.cos(angles), jnp.sin(angles)
    cos_all = jnp.concatenate([cosine, cosine], axis=1)
    sin_all = jnp.concatenate([-sine, sine], axis=1)

    token_count = SIDE * block_rows
    query_all, kv_own = call(
        qkv_kernel,
        (
            jax.ShapeDtypeStruct((token_count, 512), BF16),
            jax.ShapeDtypeStruct((token_count, 256), BF16),
        ),
        *mine,
        *theirs,
        *qkv_pieces,
        cos_all,
        sin_all,
        scalars=(qkv_offsets,),
        scratch=[
            pltpu.VMEM((token_count, width), BF16),
            pltpu.VMEM((width, 768), BF16),
        ],
        cost=(2 * token_count * width * 768, 10 << 20, 0),
        name="qkv",
    )
    kv_pieces = ring_gather(kv_own, y_shift)

    info_mine = jnp.concatenate(
        [
            piece[place * 144 + 128 : place * 144 + 129, : 2 * rows]
            for piece in qkv_pieces[:3]
            for place in range(SIDE)
        ]
        + [info_far],
        axis=0,
    )
    info_theirs = swap_cores(info_mine)
    info_mine, info_theirs = info_mine.astype(F32), info_theirs.astype(F32)
    seg_all = jnp.concatenate([info_mine[:, :rows], info_theirs[:, :rows]], axis=1)
    mod_all = jnp.concatenate([info_mine[:, rows:], info_theirs[:, rows:]], axis=1)
    pos_all = block_pos.astype(F32)
    key_info = jnp.concatenate([seg_all, jnp.where(mod_all == 1, seg_all, -2.0), pos_all], axis=0)
    query_info = jnp.stack(
        [
            seg_all[:SIDE].reshape(-1),
            jnp.where(mod_all == 1, seg_all, -1.0)[:SIDE].reshape(-1),
            pos_all[:SIDE].reshape(-1),
        ],
        axis=1,
    )
    first, last = jnp.min(seg_all, axis=1), jnp.max(seg_all, axis=1)
    q_first, q_last, q_id = first[:SIDE, None], last[:SIDE, None], block_ids[:SIDE, None]
    touches = (first[None, :] <= q_last) & (last[None, :] >= q_first)
    one_doc = (first == last)[None, :] & (q_first == q_last) & (first[None, :] == q_first)
    plain = one_doc & (block_ids[None, :] < q_id)
    kinds = jnp.where(plain, 1, jnp.where(touches, 2, 0)).astype(jnp.int32).reshape(-1)

    group = HEADS // KV_HEADS

    table = call(
        table_kernel,
        jax.ShapeDtypeStruct((512, width), BF16),
        out_all,
        scalars=(out_offsets,),
        cost=(1, 4 << 20, 0),
        name="table",
    )
    half_block = jax.ShapeDtypeStruct((rows, width), BF16)

    def attend(z_place, queries):
        return call(
            functools.partial(attend_kernel, block_rows, z_place),
            (half_block, half_block),
            queries,
            query_info,
            key_info,
            *kv_pieces,
            table,
            scalars=(kinds,),
            specs=[
                pl.BlockSpec((block_rows, 512), lambda i: (z_place, 0)),
                pl.BlockSpec((block_rows, 3), lambda i: (z_place, 0)),
                whole_block(key_info),
            ]
            + [whole_block(piece) for piece in kv_pieces]
            + [whole_block(table)],
            scratch=[
                pltpu.VMEM((16, block_rows, 256), BF16),
                pltpu.VMEM((16, group, block_rows, 256), F32),
                pltpu.VMEM((group, block_rows, HEAD_DIM), F32),
                pltpu.VMEM((group, block_rows, HEAD_DIM), F32),
                pltpu.VMEM((group, block_rows, HEAD_DIM), F32),
            ],
            cost=(4 << 30, 4 << 20, 2 << 20),
            name="attend",
        )

    sums, arrived = [], []
    queries = query_all
    for place, z_place in enumerate((3, 1, 2, 0)):
        own, other = attend(z_place, queries)
        both = own.astype(F32) + swap_cores(other).astype(F32)
        if z_place:
            both = both.astype(BF16)
            arrived.append(z_shift(both, STEPS[z_place]))
            sums.append(both)
        if place == 1:
            queries = in_order(query_all, sums[0])
        elif place == 2:
            queries = in_order(query_all, sums[1], sums[2])
    total = hidden_in.astype(F32) + both
    for part in arrived:
        total = total + part.astype(F32)
    residual = total.astype(BF16)

    normed_two = rms_normed(residual, mlp_gain)
    def weight_block(first):
        return pl.BlockSpec((16, 128, 128), lambda i: (0, first + i, 0))

    chunk = rows // 2
    chunk_count = 2 * SIDE * chunk
    out_half = jax.ShapeDtypeStruct((chunk_count // 2, width), BF16)

    def lift(mine, theirs):
        return pl.pallas_call(
            lift_kernel,
            out_shape=jax.ShapeDtypeStruct((blocks, chunk_count, 128), BF16),
            grid=(blocks,),
            in_specs=[SMEM]
            + [whole_block(piece) for piece in mine + theirs]
            + [weight_block(0), weight_block(blocks)],
            out_specs=pl.BlockSpec((1, chunk_count, 128), lambda i: (i, 0, 0)),
            scratch_shapes=[pltpu.VMEM((chunk_count, width), BF16)],
            compiler_params=pltpu.CompilerParams(vmem_limit_bytes=48 << 20),
            cost_estimate=pl.CostEstimate(
                flops=4 * chunk_count * width * hidden_units,
                bytes_accessed=10 << 20,
                transcendentals=chunk_count * hidden_units,
            ),
            name="lift",
        )(mlp_offsets, *mine, *theirs, mlp_weights, mlp_weights)

    def lower(inner):
        return pl.pallas_call(
            lower_kernel,
            out_shape=(out_half, out_half),
            grid=(width // 256,),
            in_specs=[
                SMEM,
                whole_block(inner),
                pl.BlockSpec((2, hidden_units, 128), lambda i: (i, 2, 0)),
            ],
            out_specs=(whole_block(out_half), whole_block(out_half)),
            compiler_params=pltpu.CompilerParams(vmem_limit_bytes=48 << 20),
            cost_estimate=pl.CostEstimate(
                flops=2 * chunk_count * width * hidden_units,
                bytes_accessed=8 << 20,
                transcendentals=0,
            ),
            name="lower",
        )(mlp_offsets, inner, mlp_weights)

    def spread(own, other):
        both = own.astype(F32) + swap_cores(other).astype(F32)
        parts = [
            y_shift(both[place * chunk : (place + 1) * chunk].astype(BF16), STEPS[place])
            for place in (3, 1, 2)
        ]
        return both[:chunk], parts

    def finish(start, kept, parts):
        total = residual[start : start + chunk].astype(F32) + kept
        for part in parts:
            total = total + part.astype(F32)
        return total.astype(BF16)

    first = ring_gather(normed_two[:chunk], y_shift)
    second = ring_gather(normed_two[chunk:], y_shift)
    first_inner = lift(first, [swap_cores(piece) for piece in first])
    first_inner, second = lax.optimization_barrier((first_inner, second))
    first_kept, first_parts = spread(*lower(first_inner))
    second_inner = lift(second, [swap_cores(piece) for piece in second])
    second_inner = in_order(second_inner, first_parts)
    second_kept, second_parts = spread(*lower(second_inner))
    return jnp.concatenate(
        [finish(0, first_kept, first_parts), finish(chunk, second_kept, second_parts)], axis=0
    )


def solution(mesh):
    apart = jax.sharding.Mesh(
        mesh.devices.reshape(SIDE, SIDE, SIDE, 2), ("dp", "z", "y", "tensor")
    )
    seq = ("z", "y")
    tokens = P(("dp", "z", "y", "tensor"))
    inward, outward = P(seq, "tensor"), P("tensor", seq)
    placed = (
        tokens,
        P(),
        inward,
        inward,
        inward,
        outward,
        P(),
        inward,
        inward,
        outward,
        tokens,
        tokens,
    )
    return jax.shard_map(
        per_device, mesh=apart, in_specs=placed, out_specs=tokens, check_vma=False
    )
```

```python
import functools

import jax
import jax.numpy as jnp
from jax import lax
from jax.experimental import pallas as pl
from jax.experimental.pallas import tpu as pltpu
from jax.sharding import PartitionSpec as P

HEADS = 32
KV_HEADS = 8
HEAD_DIM = 128
EPSILON = 1e-05
THETA = 500000.0
SIDE = 4
BF16 = jnp.bfloat16
F32 = jnp.float32
SMEM = pl.BlockSpec(memory_space=pltpu.SMEM)
STEPS = (0, -1, 1, 2)


def x_shift(value, step):
    return lax.ppermute(value, "dp", [(i, (i + step) % SIDE) for i in range(SIDE)])


def y_shift(value, step):
    return lax.ppermute(value, "y", [(i, (i + step) % SIDE) for i in range(SIDE)])


def z_shift(value, step):
    return lax.ppermute(value, "z", [(i, (i + step) % SIDE) for i in range(SIDE)])


def plane_shift(value):
    return lax.ppermute(
        value,
        ("dp", "y"),
        [(x * SIDE + (y + x) % SIDE, x * SIDE + y) for x in range(1, SIDE) for y in range(SIDE)],
    )


def swap_cores(value):
    return lax.ppermute(value, "tensor", [(0, 1), (1, 0)])


def ring_gather(value, shift):
    return [value if step == 0 else shift(value, -step) for step in STEPS]


def relay_gather(value, shift):
    half = value.shape[0] // 2
    before, after = shift(value, 1), shift(value, -1)
    return [value, before, after, shift(after[:half], -1), shift(before[half:], 1)]


def in_order(values, *earlier):
    kept = lax.optimization_barrier((values, earlier))
    return kept[0]


def place_tokens(mine, theirs, whole):
    rows, width = mine[0].shape[0], whole.shape[1]
    for which, pieces in enumerate((mine, theirs)):
        for place in range(SIDE):
            start = (2 * place + which) * rows
            for piece in pieces[place : None if place == 3 else place + 1]:
                whole[start : start + piece.shape[0], :] = piece[:, piece.shape[1] - width :]
                start += piece.shape[0]


def plane_blocks(pieces, rows):
    for piece in pieces:
        for start in range(0, piece.shape[0], rows):
            yield piece, start


def cut_kernel(places, query, key, value, info, *parts):
    rows = query.shape[0]
    for turn in range(SIDE):
        place, part = places[turn], parts[turn]
        wide, narrow = pl.multiple_of(place * 512, 512), pl.multiple_of(place * 128, 128)
        part[:rows, :512] = query[:, pl.ds(wide, 512)]
        part[:rows, 512:640] = key[:, pl.ds(narrow, 128)]
        part[:rows, 640:] = value[:, pl.ds(narrow, 128)]
        part[rows:, :] = info[...]


def norm_kernel(places, hidden, gain, out, gate, up, down, *refs):
    parts, packed = refs[:-1], refs[-1]
    normed = rms_normed(hidden[...], gain[...])
    for turn in range(SIDE):
        place, part = places[turn], parts[turn]
        for block in range(0, 512, 128):
            part[:, block : block + 128] = out[
                pl.ds(pl.multiple_of(place * 512 + block, 128), 128), :
            ]
        if part.shape[1] > 512:
            part[:, 512:] = normed
    units = gate.shape[1]
    for block in range(units // 128):
        start = block * 128
        packed[start : start + 128, :] = gate[:, start : start + 128]
        packed[units + start : units + start + 128, :] = up[:, start : start + 128]
    packed[2 * units :, :] = down[...]


def rms_normed(values, gain_vec):
    widened = values.astype(F32)
    mean_square = jnp.mean(widened * widened, axis=-1, keepdims=True)
    return (widened * lax.rsqrt(mean_square + EPSILON) * gain_vec).astype(BF16)


def qkv_kernel(offsets, *refs):
    mine, theirs, weights = refs[0:5], refs[5:10], refs[10:15]
    cosine, sine, query_out, kv_out, tokens, table = refs[15:]
    place_tokens(mine, theirs, tokens)
    depth = 128
    for slot, (source, start) in enumerate(plane_blocks(weights, weights[0].shape[0] // SIDE)):
        row = pl.multiple_of(offsets[slot], depth)
        table[pl.ds(row, depth), :] = source[start : start + depth, :]
    cos_all, sin_all = cosine[...], sine[...]

    def rotated(part):
        return part * cos_all + pltpu.roll(part, HEAD_DIM // 2, 1) * sin_all

    for block in range(3):
        sums = jnp.dot(
            tokens[...], table[:, block * 256 : block * 256 + 256], preferred_element_type=F32
        )
        first, second = sums[:, :HEAD_DIM], sums[:, HEAD_DIM:]
        if block < 2:
            query_out[:, block * 256 : block * 256 + HEAD_DIM] = rotated(first).astype(BF16)
            query_out[:, block * 256 + HEAD_DIM : block * 256 + 256] = rotated(second).astype(BF16)
        else:
            kv_out[:, :HEAD_DIM] = rotated(first).astype(BF16)
            kv_out[:, HEAD_DIM:] = second.astype(BF16)


def attend_kernel(block_rows, kinds, query, query_info, key_info, *refs):
    kv_pieces = refs[0:4]
    out, kv_all, scores, top, total, mixed = refs[4:]
    z_place = pl.program_id(0)
    group = HEADS // KV_HEADS
    scale = HEAD_DIM**-0.5 * 1.4426950408889634

    @pl.when(z_place == 0)
    def _():
        for slot in range(16):
            start = slot % SIDE * block_rows
            kv_all[slot] = kv_pieces[slot // SIDE][start : start + block_rows, :]

    top[...] = jnp.full(top.shape, -1e30, F32)
    total[...] = jnp.zeros_like(total)
    mixed[...] = jnp.zeros_like(mixed)

    def score_of(head, key):
        return lax.dot_general(
            query[:, head * HEAD_DIM : (head + 1) * HEAD_DIM],
            key,
            (((1,), (1,)), ((), ())),
            preferred_element_type=F32,
        )

    def keep(slot, head, score):
        scores[slot, head] = score
        top[head] = jnp.maximum(
            top[head], jnp.maximum(score[:, :HEAD_DIM], score[:, HEAD_DIM:])
        )

    def first_pass(slot, carry):
        kind = kinds[z_place * 16 + slot]

        @pl.when(kind == 1)
        def _():
            key = kv_all[slot, :, :HEAD_DIM]
            for head in range(group):
                keep(slot, head, score_of(head, key))

        @pl.when(kind == 2)
        def _():
            key = kv_all[slot, :, :HEAD_DIM]
            key_seg = key_info[pl.ds(slot, 1), :]
            key_video = key_info[pl.ds(16 + slot, 1), :]
            key_pos = key_info[pl.ds(32 + slot, 1), :]
            same = query_info[:, 0:1] == key_seg
            video = query_info[:, 1:2] == key_video
            earlier = key_pos <= query_info[:, 2:3]
            allowed = video | (same & earlier)
            for head in range(group):
                keep(slot, head, jnp.where(allowed, score_of(head, key), -1e30))

        return carry

    lax.fori_loop(0, 16, first_pass, 0)
    for head in range(group):
        top[head] = jnp.broadcast_to(
            jnp.max(top[head], axis=-1, keepdims=True), top.shape[1:]
        )

    def second_pass(slot, carry):
        @pl.when(kinds[z_place * 16 + slot] > 0)
        def _():
            value = kv_all[slot, :, HEAD_DIM:]
            for head in range(group):
                high = top[head]
                left = jnp.exp2((scores[slot, head, :, :HEAD_DIM] - high) * scale)
                right = jnp.exp2((scores[slot, head, :, HEAD_DIM:] - high) * scale)
                total[head] = total[head] + (left + right)
                terms = jnp.concatenate([left.astype(BF16), right.astype(BF16)], axis=1)
                mixed[head] = mixed[head] + jnp.dot(terms, value, preferred_element_type=F32)

        return carry

    lax.fori_loop(0, 16, second_pass, 0)
    for head in range(group):
        out[:, head * HEAD_DIM : (head + 1) * HEAD_DIM] = (
            mixed[head] / jnp.sum(total[head], axis=-1, keepdims=True)
        ).astype(BF16)


def table_kernel(offsets, *refs):
    pieces, table = refs[:-1], refs[-1]
    for slot, (source, start) in enumerate(plane_blocks(pieces, 128)):
        column = pl.multiple_of(offsets[slot], 128)
        for block in range(0, 512, 128):
            table[block : block + 128, pl.ds(column, 128)] = source[
                start : start + 128, block : block + 128
            ]


def project_kernel(attended, table, own_out, other_out):
    half = own_out.shape[0]
    for start in range(0, table.shape[1], 512):
        part = jnp.dot(
            attended[...], table[:, start : start + 512], preferred_element_type=F32
        ).astype(BF16)
        own_out[:, start : start + 512] = part[:half]
        other_out[:, start : start + 512] = part[half:]


def lift_kernel(order, *refs):
    mine, theirs = refs[0:4], refs[4:8]
    gate, up, inner, tokens = refs[8:]

    @pl.when(pl.program_id(0) == 0)
    def _():
        place_tokens(mine, theirs, tokens)

    pair = jnp.concatenate(
        [
            jnp.concatenate([gate[order[block]], up[order[block]]], axis=1)
            for block in range(16)
        ],
        axis=0,
    )
    sums = jnp.dot(tokens[...], pair, preferred_element_type=F32)
    gated, lifted = sums[:, :128], sums[:, 128:]
    inner[0] = (gated / (1.0 + jnp.exp(-gated)) * lifted).astype(BF16)


def lower_kernel(order, inner, down_left, down_right, own_out, other_out):
    blocks, rows = inner.shape[0], inner.shape[1]
    lhs = jnp.concatenate([inner[block] for block in range(blocks)], axis=1)
    rhs = jnp.concatenate([down_left[0], down_right[0]], axis=1)
    part = jnp.dot(lhs, rhs, preferred_element_type=F32).astype(BF16)
    part = part.reshape(SIDE, 2, rows // 8, 256)
    own_out[...] = part[:, 0].reshape(rows // 2, 256)
    other_out[...] = part[:, 1].reshape(rows // 2, 256)


def whole_block(array):
    return pl.BlockSpec(array.shape, lambda *step: (0,) * array.ndim)


def call(kernel, out_shape, *operands, scalars=(), specs=None, scratch=(), cost=(1, 1, 0), name):
    specs = [whole_block(array) for array in operands] if specs is None else specs
    return pl.pallas_call(
        kernel,
        out_shape=out_shape,
        grid=(1,),
        in_specs=[SMEM] * len(scalars) + specs,
        out_specs=jax.tree.map(whole_block, out_shape),
        scratch_shapes=list(scratch),
        compiler_params=pltpu.CompilerParams(vmem_limit_bytes=48 << 20),
        cost_estimate=pl.CostEstimate(
            flops=cost[0], bytes_accessed=cost[1], transcendentals=cost[2]
        ),
        name=name,
    )(*scalars, *operands)


def per_device(
    hidden_in,
    attn_gain,
    query_weight,
    key_weight,
    value_weight,
    out_weight,
    mlp_gain,
    gate_weight,
    up_weight,
    down_weight,
    segment_ids,
    modality,
):
    x, z, y = lax.axis_index("dp"), lax.axis_index("z"), lax.axis_index("y")
    core = lax.axis_index("tensor")
    rows, width = hidden_in.shape
    block_rows = 2 * rows
    z_places = [(z + step) % SIDE for step in STEPS]
    y_places = [(y + step) % SIDE for step in STEPS]
    block_ids = jnp.stack([zz * SIDE + yy for yy in y_places for zz in z_places]).astype(jnp.int32)
    info = jnp.concatenate([segment_ids, modality]).astype(BF16).reshape(1, 2 * rows)
    info_rows = jnp.pad(info, ((0, 15), (0, 768 - 2 * rows)))

    hidden_units = gate_weight.shape[1] // SIDE
    blocks = hidden_units // 128
    places = jnp.stack([(z - step) % SIDE for step in STEPS] + [(y - x) % SIDE]).astype(jnp.int32)

    def cut(kernel, shapes, whole, units, name):
        outs = [jax.ShapeDtypeStruct(shape, BF16) for shape in shapes]
        quarters = [
            pl.BlockSpec((128, hidden_units), lambda i, place: (0, place[SIDE])),
            pl.BlockSpec((128, hidden_units), lambda i, place: (0, place[SIDE])),
            pl.BlockSpec((hidden_units, 128), lambda i, place: (place[SIDE], 0)),
        ]
        return pl.pallas_call(
            kernel,
            out_shape=outs,
            grid_spec=pltpu.PrefetchScalarGridSpec(
                num_scalar_prefetch=1,
                grid=(1,),
                in_specs=[whole_block(array) for array in whole] + quarters[: len(units)],
                out_specs=[whole_block(out) for out in outs],
            ),
            compiler_params=pltpu.CompilerParams(vmem_limit_bytes=58 << 20),
            cost_estimate=pl.CostEstimate(flops=1, bytes_accessed=4 << 20, transcendentals=0),
            name=name,
        )(places, *whole, *units)

    def from_ring(parts):
        return [part if step == 0 else z_shift(part, -step) for part, step in zip(parts, STEPS)]

    qkv_parts = cut(
        cut_kernel,
        [(rows + 16, 768)] * SIDE,
        [query_weight, key_weight, value_weight, info_rows],
        [],
        "cut",
    )
    qkv_ring = from_ring(qkv_parts)
    qkv_pieces = relay_gather(jnp.concatenate(qkv_ring, axis=0), y_shift)

    hidden, _ = lax.optimization_barrier((hidden_in, qkv_parts))
    *token_parts, mlp_own = cut(
        norm_kernel,
        [(rows, 512 + width)] * 3 + [(rows, 512), (3 * hidden_units, 128)],
        [hidden, attn_gain.reshape(1, width), out_weight],
        [gate_weight, up_weight, down_weight],
        "norm",
    )
    token_ring = from_ring(token_parts)
    half = rows // 2
    mine = token_ring[:3] + [
        z_shift(token_ring[2][:half, 512:], -1),
        z_shift(token_ring[1][half:, 512:], 1),
    ]
    theirs = [swap_cores(piece) for piece in mine]
    mlp_moved = in_order(plane_shift(mlp_own), mine, qkv_pieces[1:3])
    mlp_part = jnp.where(x == 0, mlp_own, mlp_moved)
    mine, theirs, qkv_pieces = lax.optimization_barrier((mine, theirs, qkv_pieces))

    mlp_weights = lax.all_gather(mlp_part, ("dp", "z"), axis=0, tiled=False)
    mlp_order = jnp.stack(
        [(yy - y) % SIDE * SIDE + zz for zz in range(SIDE) for yy in range(SIDE)]
    ).astype(jnp.int32)

    in_block = (jnp.arange(block_rows, dtype=jnp.int32) + core * rows) % block_rows
    block_pos = block_ids[:, None] * block_rows + in_block[None, :]
    half_dim = HEAD_DIM // 2
    inverse_freq = THETA ** (-2.0 * jnp.arange(half_dim, dtype=F32) / HEAD_DIM)
    angles = block_pos[:SIDE].reshape(-1).astype(F32)[:, None] * inverse_freq[None, :]
    cosine, sine = jnp.cos(angles), jnp.sin(angles)
    cos_all = jnp.concatenate([cosine, cosine], axis=1)
    sin_all = jnp.concatenate([-sine, sine], axis=1)

    token_count = SIDE * block_rows
    query_all, kv_own = call(
        qkv_kernel,
        (
            jax.ShapeDtypeStruct((token_count, 512), BF16),
            jax.ShapeDtypeStruct((token_count, 256), BF16),
        ),
        *mine,
        *theirs,
        *qkv_pieces,
        cos_all,
        sin_all,
        scalars=(block_ids * 128,),
        scratch=[
            pltpu.VMEM((token_count, width), BF16),
            pltpu.VMEM((width, 768), BF16),
        ],
        cost=(2 * token_count * width * 768, 10 << 20, 0),
        name="qkv",
    )
    kv_pieces = ring_gather(kv_own, y_shift)

    qkv_pieces = in_order(qkv_pieces, query_all)
    info_mine = jnp.concatenate(
        [
            piece[start + rows : start + rows + 1, : 2 * rows]
            for piece, start in plane_blocks(qkv_pieces, rows + 16)
        ],
        axis=0,
    )
    info_theirs = swap_cores(info_mine)
    info_mine, info_theirs = info_mine.astype(F32), info_theirs.astype(F32)
    seg_all = jnp.concatenate([info_mine[:, :rows], info_theirs[:, :rows]], axis=1)
    mod_all = jnp.concatenate([info_mine[:, rows:], info_theirs[:, rows:]], axis=1)
    pos_all = block_pos.astype(F32)
    key_info = jnp.concatenate([seg_all, jnp.where(mod_all == 1, seg_all, -2.0), pos_all], axis=0)
    query_info = jnp.stack(
        [
            seg_all[:SIDE].reshape(-1),
            jnp.where(mod_all == 1, seg_all, -1.0)[:SIDE].reshape(-1),
            pos_all[:SIDE].reshape(-1),
        ],
        axis=1,
    )
    first, last = jnp.min(seg_all, axis=1), jnp.max(seg_all, axis=1)
    q_first, q_last, q_id = first[:SIDE, None], last[:SIDE, None], block_ids[:SIDE, None]
    touches = (first[None, :] <= q_last) & (last[None, :] >= q_first)
    one_doc = (first == last)[None, :] & (q_first == q_last) & (first[None, :] == q_first)
    plain = one_doc & (block_ids[None, :] < q_id)
    kinds = jnp.where(plain, 1, jnp.where(touches, 2, 0)).astype(jnp.int32).reshape(-1)

    group = HEADS // KV_HEADS

    info_block = pl.BlockSpec((block_rows, 3), lambda i: (i, 0))
    head_block = pl.BlockSpec((block_rows, 512), lambda i: (i, 0))
    attended = pl.pallas_call(
        functools.partial(attend_kernel, block_rows),
        out_shape=jax.ShapeDtypeStruct((token_count, 512), BF16),
        grid=(SIDE,),
        in_specs=[SMEM, head_block, info_block, whole_block(key_info)]
        + [whole_block(piece) for piece in kv_pieces],
        out_specs=head_block,
        scratch_shapes=[
            pltpu.VMEM((16, block_rows, 256), BF16),
            pltpu.VMEM((16, group, block_rows, 256), F32),
            pltpu.VMEM((group, block_rows, HEAD_DIM), F32),
            pltpu.VMEM((group, block_rows, HEAD_DIM), F32),
            pltpu.VMEM((group, block_rows, HEAD_DIM), F32),
        ],
        compiler_params=pltpu.CompilerParams(vmem_limit_bytes=48 << 20),
        cost_estimate=pl.CostEstimate(
            flops=16 << 30, bytes_accessed=6 << 20, transcendentals=8 << 20
        ),
        name="attend",
    )(kinds, query_all, query_info, key_info, *kv_pieces)

    out_plane = jnp.concatenate([part[:, :512] for part in token_ring], axis=0)
    out_pieces = ring_gather(in_order(out_plane, kv_pieces), y_shift)
    table = call(
        table_kernel,
        jax.ShapeDtypeStruct((512, width), BF16),
        *out_pieces,
        scalars=(block_ids * 128,),
        cost=(1, 4 << 20, 0),
        name="table",
    )
    half_block = jax.ShapeDtypeStruct((rows, width), BF16)

    sums, arrived = [], []
    for place, z_place in enumerate((3, 1, 2, 0)):
        given = attended if place < 2 else in_order(attended, sums[place - 2])
        own, other = call(
            project_kernel,
            (half_block, half_block),
            given,
            table,
            specs=[
                pl.BlockSpec((block_rows, 512), lambda i, z_place=z_place: (z_place, 0)),
                whole_block(table),
            ],
            cost=(2 * block_rows * 512 * width, 4 << 20, 0),
            name="project",
        )
        both = own.astype(F32) + swap_cores(other).astype(F32)
        if z_place:
            both = both.astype(BF16)
            arrived.append(z_shift(both, STEPS[z_place]))
            sums.append(both)
    total = hidden_in.astype(F32) + both
    for part in arrived:
        total = total + part.astype(F32)
    residual = total.astype(BF16)

    normed_two = rms_normed(residual, mlp_gain)
    def weight_block(first):
        return pl.BlockSpec((16, 128, 128), lambda i: (0, first + i, 0))

    chunk = rows
    chunk_count = 2 * SIDE * chunk
    out_half = jax.ShapeDtypeStruct((chunk_count // 2, width), BF16)

    def lift(mine, theirs):
        return pl.pallas_call(
            lift_kernel,
            out_shape=jax.ShapeDtypeStruct((blocks, chunk_count, 128), BF16),
            grid=(blocks,),
            in_specs=[SMEM]
            + [whole_block(piece) for piece in mine + theirs]
            + [weight_block(0), weight_block(blocks)],
            out_specs=pl.BlockSpec((1, chunk_count, 128), lambda i: (i, 0, 0)),
            scratch_shapes=[pltpu.VMEM((chunk_count, width), BF16)],
            compiler_params=pltpu.CompilerParams(vmem_limit_bytes=48 << 20),
            cost_estimate=pl.CostEstimate(
                flops=4 * chunk_count * width * hidden_units,
                bytes_accessed=10 << 20,
                transcendentals=chunk_count * hidden_units,
            ),
            name="lift",
        )(mlp_order, *mine, *theirs, mlp_weights, mlp_weights)

    def lower(inner):
        def down_block(side):
            return pl.BlockSpec(
                (1, hidden_units, 128), lambda i, order: (order[2 * i + side], 2, 0)
            )

        out_block = pl.BlockSpec((chunk_count // 2, 256), lambda i, order: (0, i))
        return pl.pallas_call(
            lower_kernel,
            out_shape=(out_half, out_half),
            grid_spec=pltpu.PrefetchScalarGridSpec(
                num_scalar_prefetch=1,
                grid=(width // 256,),
                in_specs=[whole_block(inner), down_block(0), down_block(1)],
                out_specs=(out_block, out_block),
            ),
            compiler_params=pltpu.CompilerParams(vmem_limit_bytes=48 << 20),
            cost_estimate=pl.CostEstimate(
                flops=2 * chunk_count * width * hidden_units,
                bytes_accessed=8 << 20,
                transcendentals=0,
            ),
            name="lower",
        )(mlp_order, inner, mlp_weights, mlp_weights)

    def spread(own, other):
        both = own.astype(F32) + swap_cores(other).astype(F32)
        parts = [
            y_shift(both[place * chunk : (place + 1) * chunk].astype(BF16), STEPS[place])
            for place in (3, 1, 2)
        ]
        return both[:chunk], parts

    def finish(start, kept, parts):
        total = residual[start : start + chunk].astype(F32) + kept
        for part in parts:
            total = total + part.astype(F32)
        return total.astype(BF16)

    mine = ring_gather(normed_two, y_shift)
    kept, parts = spread(*lower(lift(mine, [swap_cores(piece) for piece in mine])))
    return finish(0, kept, parts)


def solution(mesh):
    apart = jax.sharding.Mesh(
        mesh.devices.reshape(SIDE, SIDE, SIDE, 2), ("dp", "z", "y", "tensor")
    )
    seq = ("z", "y")
    tokens = P(("dp", "z", "y", "tensor"))
    inward, outward = P(seq, "tensor"), P("tensor", seq)
    placed = (
        tokens,
        P(),
        inward,
        inward,
        inward,
        outward,
        P(),
        inward,
        inward,
        outward,
        tokens,
        tokens,
    )
    return jax.shard_map(
        per_device, mesh=apart, in_specs=placed, out_specs=tokens, check_vma=False
    )
```

```python
import functools

import jax
import jax.numpy as jnp
from jax import lax
from jax.experimental import pallas as pl
from jax.experimental.pallas import tpu as pltpu
from jax.sharding import PartitionSpec as P

HEADS = 32
KV_HEADS = 8
HEAD_DIM = 128
EPSILON = 1e-05
THETA = 500000.0
SIDE = 4
BF16 = jnp.bfloat16
F32 = jnp.float32
SMEM = pl.BlockSpec(memory_space=pltpu.SMEM)
STEPS = (0, -1, 1, 2)


def x_shift(value, step):
    return lax.ppermute(value, "dp", [(i, (i + step) % SIDE) for i in range(SIDE)])


def y_shift(value, step):
    return lax.ppermute(value, "y", [(i, (i + step) % SIDE) for i in range(SIDE)])


def z_shift(value, step):
    return lax.ppermute(value, "z", [(i, (i + step) % SIDE) for i in range(SIDE)])


def plane_shift(value):
    return lax.ppermute(
        value,
        ("dp", "y"),
        [(x * SIDE + (y + x) % SIDE, x * SIDE + y) for x in range(1, SIDE) for y in range(SIDE)],
    )


def swap_cores(value):
    return lax.ppermute(value, "tensor", [(0, 1), (1, 0)])


def ring_gather(value, shift):
    return [value if step == 0 else shift(value, -step) for step in STEPS]


def relay_gather(value, shift, *earlier):
    half = value.shape[0] // 2
    before, after = shift(value, 1), shift(value, -1)
    low, high = in_order((after[:half], before[half:]), *earlier)
    return [value, before, after, shift(low, -1), shift(high, 1)]


def in_order(values, *earlier):
    kept = lax.optimization_barrier((values, earlier))
    return kept[0]


def place_tokens(mine, theirs, whole):
    rows, width = mine[0].shape[0], whole.shape[1]
    for which, pieces in enumerate((mine, theirs)):
        for place in range(SIDE):
            start = (2 * place + which) * rows
            for piece in pieces[place : None if place == 3 else place + 1]:
                whole[start : start + piece.shape[0], :] = piece[:, piece.shape[1] - width :]
                start += piece.shape[0]


def plane_blocks(pieces, rows):
    for piece in pieces:
        for start in range(0, piece.shape[0], rows):
            yield piece, start


def cut_kernel(places, query, key, value, segments, modes, gate, up, down, *refs):
    parts, packed = refs[:-1], refs[-1]
    rows = query.shape[0]
    for turn in range(SIDE):
        place, part = places[turn], parts[turn]
        wide, narrow = pl.multiple_of(place * 512, 512), pl.multiple_of(place * 128, 128)
        part[:rows, :512] = query[:, pl.ds(wide, 512)]
        part[:rows, 512:640] = key[:, pl.ds(narrow, 128)]
        part[:rows, 640:] = value[:, pl.ds(narrow, 128)]
        below = part.shape[0] - rows
        for start, row in ((0, segments), (rows, modes)):
            part[rows:, start : start + rows] = jnp.broadcast_to(
                row[...].astype(F32), (below, rows)
            ).astype(BF16)
        part[rows:, 2 * rows :] = jnp.zeros((below, part.shape[1] - 2 * rows), BF16)
    units = gate.shape[1]
    for block in range(units // 128):
        start = block * 128
        packed[start : start + 128, :] = gate[:, start : start + 128]
        packed[units + start : units + start + 128, :] = up[:, start : start + 128]
    packed[2 * units :, :] = down[...]


def norm_kernel(places, hidden, gain, out, *parts):
    normed = rms_normed(hidden[...], gain[...])
    for turn in range(SIDE):
        place, part = places[turn], parts[turn]
        for block in range(0, 512, 128):
            part[:, block : block + 128] = out[
                pl.ds(pl.multiple_of(place * 512 + block, 128), 128), :
            ]
        if part.shape[1] > 512:
            part[:, 512:] = normed


def rms_normed(values, gain_vec):
    widened = values.astype(F32)
    mean_square = jnp.mean(widened * widened, axis=-1, keepdims=True)
    return (widened * lax.rsqrt(mean_square + EPSILON) * gain_vec).astype(BF16)


def qkv_kernel(offsets, *refs):
    mine, theirs, weights = refs[0:5], refs[5:10], refs[10:15]
    cosine, sine, query_out, kv_out, tokens, table = refs[15:]
    place_tokens(mine, theirs, tokens)
    depth = 128
    for slot, (source, start) in enumerate(plane_blocks(weights, weights[0].shape[0] // SIDE)):
        row = pl.multiple_of(offsets[slot], depth)
        table[pl.ds(row, depth), :] = source[start : start + depth, :]
    cos_all, sin_all = cosine[...], sine[...]

    def rotated(part):
        return part * cos_all + pltpu.roll(part, HEAD_DIM // 2, 1) * sin_all

    for block in range(3):
        sums = jnp.dot(
            tokens[...], table[:, block * 256 : block * 256 + 256], preferred_element_type=F32
        )
        first, second = sums[:, :HEAD_DIM], sums[:, HEAD_DIM:]
        if block < 2:
            query_out[:, block * 256 : block * 256 + HEAD_DIM] = rotated(first).astype(BF16)
            query_out[:, block * 256 + HEAD_DIM : block * 256 + 256] = rotated(second).astype(BF16)
        else:
            kv_out[:, :HEAD_DIM] = rotated(first).astype(BF16)
            kv_out[:, HEAD_DIM:] = second.astype(BF16)


def attend_kernel(block_rows, kinds, query, query_info, key_info, *refs):
    kv_pieces = refs[0:5]
    out, kv_all, scores, top, total, mixed = refs[5:]
    z_place = pl.program_id(0)
    group = HEADS // KV_HEADS
    scale = HEAD_DIM**-0.5 * 1.4426950408889634

    @pl.when(z_place == 0)
    def _():
        for slot, (source, start) in enumerate(plane_blocks(kv_pieces, block_rows)):
            kv_all[slot] = source[start : start + block_rows, :]

    top[...] = jnp.full(top.shape, -1e30, F32)
    total[...] = jnp.zeros_like(total)
    mixed[...] = jnp.zeros_like(mixed)

    def score_of(head, key):
        return lax.dot_general(
            query[:, head * HEAD_DIM : (head + 1) * HEAD_DIM],
            key,
            (((1,), (1,)), ((), ())),
            preferred_element_type=F32,
        )

    def keep(slot, head, score):
        scores[slot, head] = score
        top[head] = jnp.maximum(
            top[head], jnp.maximum(score[:, :HEAD_DIM], score[:, HEAD_DIM:])
        )

    def first_pass(slot, carry):
        kind = kinds[z_place * 16 + slot]

        @pl.when(kind == 1)
        def _():
            key = kv_all[slot, :, :HEAD_DIM]
            for head in range(group):
                keep(slot, head, score_of(head, key))

        @pl.when(kind == 2)
        def _():
            key = kv_all[slot, :, :HEAD_DIM]
            key_seg = key_info[pl.ds(slot, 1), :]
            key_video = key_info[pl.ds(16 + slot, 1), :]
            key_pos = key_info[pl.ds(32 + slot, 1), :]
            same = query_info[:, 0:1] == key_seg
            video = query_info[:, 1:2] == key_video
            earlier = key_pos <= query_info[:, 2:3]
            allowed = video | (same & earlier)
            for head in range(group):
                keep(slot, head, jnp.where(allowed, score_of(head, key), -1e30))

        return carry

    lax.fori_loop(0, 16, first_pass, 0)
    for head in range(group):
        top[head] = jnp.broadcast_to(
            jnp.max(top[head], axis=-1, keepdims=True), top.shape[1:]
        )

    def second_pass(slot, carry):
        @pl.when(kinds[z_place * 16 + slot] > 0)
        def _():
            value = kv_all[slot, :, HEAD_DIM:]
            for head in range(group):
                high = top[head]
                left = jnp.exp2((scores[slot, head, :, :HEAD_DIM] - high) * scale)
                right = jnp.exp2((scores[slot, head, :, HEAD_DIM:] - high) * scale)
                total[head] = total[head] + (left + right)
                terms = jnp.concatenate([left.astype(BF16), right.astype(BF16)], axis=1)
                mixed[head] = mixed[head] + jnp.dot(terms, value, preferred_element_type=F32)

        return carry

    lax.fori_loop(0, 16, second_pass, 0)
    for head in range(group):
        out[:, head * HEAD_DIM : (head + 1) * HEAD_DIM] = (
            mixed[head] / jnp.sum(total[head], axis=-1, keepdims=True)
        ).astype(BF16)


def table_kernel(offsets, *refs):
    pieces, table = refs[:-1], refs[-1]
    for slot, (source, start) in enumerate(plane_blocks(pieces, 128)):
        column = pl.multiple_of(offsets[slot], 128)
        for block in range(0, 512, 128):
            table[block : block + 128, pl.ds(column, 128)] = source[
                start : start + 128, block : block + 128
            ]


def project_kernel(attended, table, own_out, other_out):
    half = own_out.shape[0]
    for start in range(0, table.shape[1], 512):
        part = jnp.dot(
            attended[...], table[:, start : start + 512], preferred_element_type=F32
        ).astype(BF16)
        own_out[:, start : start + 512] = part[:half]
        other_out[:, start : start + 512] = part[half:]


def lift_kernel(order, *refs):
    mine, theirs = refs[0:5], refs[5:10]
    gate, up, inner, tokens = refs[10:]

    @pl.when(pl.program_id(0) == 0)
    def _():
        place_tokens(mine, theirs, tokens)

    pair = jnp.concatenate(
        [
            jnp.concatenate([gate[order[block]], up[order[block]]], axis=1)
            for block in range(16)
        ],
        axis=0,
    )
    sums = jnp.dot(tokens[...], pair, preferred_element_type=F32)
    gated, lifted = sums[:, :128], sums[:, 128:]
    inner[0] = (gated / (1.0 + jnp.exp(-gated)) * lifted).astype(BF16)


def lower_kernel(order, inner, down_left, down_right, own_out, other_out):
    blocks, rows = inner.shape[0], inner.shape[1]
    lhs = jnp.concatenate([inner[block] for block in range(blocks)], axis=1)
    rhs = jnp.concatenate([down_left[0], down_right[0]], axis=1)
    part = jnp.dot(lhs, rhs, preferred_element_type=F32).astype(BF16)
    part = part.reshape(SIDE, 2, rows // 8, 256)
    own_out[...] = part[:, 0].reshape(rows // 2, 256)
    other_out[...] = part[:, 1].reshape(rows // 2, 256)


def whole_block(array):
    return pl.BlockSpec(array.shape, lambda *step: (0,) * array.ndim)


def call(kernel, out_shape, *operands, scalars=(), specs=None, scratch=(), cost=(1, 1, 0), name):
    specs = [whole_block(array) for array in operands] if specs is None else specs
    return pl.pallas_call(
        kernel,
        out_shape=out_shape,
        grid=(1,),
        in_specs=[SMEM] * len(scalars) + specs,
        out_specs=jax.tree.map(whole_block, out_shape),
        scratch_shapes=list(scratch),
        compiler_params=pltpu.CompilerParams(vmem_limit_bytes=48 << 20),
        cost_estimate=pl.CostEstimate(
            flops=cost[0], bytes_accessed=cost[1], transcendentals=cost[2]
        ),
        name=name,
    )(*scalars, *operands)


def per_device(
    hidden_in,
    attn_gain,
    query_weight,
    key_weight,
    value_weight,
    out_weight,
    mlp_gain,
    gate_weight,
    up_weight,
    down_weight,
    segment_ids,
    modality,
):
    x, z, y = lax.axis_index("dp"), lax.axis_index("z"), lax.axis_index("y")
    core = lax.axis_index("tensor")
    rows, width = hidden_in.shape
    block_rows = 2 * rows
    z_places = [(z + step) % SIDE for step in STEPS]
    y_places = [(y + step) % SIDE for step in STEPS]
    block_ids = jnp.stack([zz * SIDE + yy for yy in y_places for zz in z_places]).astype(jnp.int32)
    hidden_units = gate_weight.shape[1] // SIDE
    blocks = hidden_units // 128
    places = jnp.stack([(z - step) % SIDE for step in STEPS] + [(y - x) % SIDE]).astype(jnp.int32)

    def cut(kernel, shapes, whole, units, name):
        outs = [jax.ShapeDtypeStruct(shape, BF16) for shape in shapes]
        quarters = [
            pl.BlockSpec((128, hidden_units), lambda i, place: (0, place[SIDE])),
            pl.BlockSpec((128, hidden_units), lambda i, place: (0, place[SIDE])),
            pl.BlockSpec((hidden_units, 128), lambda i, place: (place[SIDE], 0)),
        ]
        return pl.pallas_call(
            kernel,
            out_shape=outs,
            grid_spec=pltpu.PrefetchScalarGridSpec(
                num_scalar_prefetch=1,
                grid=(1,),
                in_specs=[whole_block(array) for array in whole] + quarters[: len(units)],
                out_specs=[whole_block(out) for out in outs],
            ),
            compiler_params=pltpu.CompilerParams(vmem_limit_bytes=58 << 20),
            cost_estimate=pl.CostEstimate(flops=1, bytes_accessed=4 << 20, transcendentals=0),
            name=name,
        )(places, *whole, *units)

    def from_ring(parts):
        return [part if step == 0 else z_shift(part, -step) for part, step in zip(parts, STEPS)]

    in_block = (jnp.arange(block_rows, dtype=jnp.int32) + core * rows) % block_rows
    block_pos = block_ids[:, None] * block_rows + in_block[None, :]
    half_dim = HEAD_DIM // 2
    inverse_freq = THETA ** (-2.0 * jnp.arange(half_dim, dtype=F32) / HEAD_DIM)
    angles = block_pos[:SIDE].reshape(-1).astype(F32)[:, None] * inverse_freq[None, :]
    cosine, sine = jnp.cos(angles), jnp.sin(angles)
    cos_all = jnp.concatenate([cosine, cosine], axis=1)
    sin_all = jnp.concatenate([-sine, sine], axis=1)

    *qkv_parts, mlp_own = cut(
        cut_kernel,
        [(rows + 16, 768)] * SIDE + [(3 * hidden_units, 128)],
        [
            query_weight,
            key_weight,
            value_weight,
            segment_ids.reshape(1, rows),
            modality.reshape(1, rows),
        ],
        [gate_weight, up_weight, down_weight],
        "cut",
    )
    qkv_ring = from_ring(qkv_parts)
    mlp_moved = plane_shift(mlp_own)
    qkv_plane = jnp.concatenate(qkv_ring, axis=0)

    hidden, _ = lax.optimization_barrier((hidden_in, qkv_parts))
    token_parts = cut(
        norm_kernel,
        [(rows, 512 + width)] * 3 + [(rows, 512)],
        [hidden, attn_gain.reshape(1, width), out_weight],
        [],
        "norm",
    )
    token_ring = from_ring(token_parts[:3])
    qkv_plane = in_order(qkv_plane, mlp_moved, token_parts, cos_all, sin_all)
    half = rows // 2
    mine = token_ring[:3] + [
        z_shift(token_ring[2][:half, 512:], -1),
        z_shift(token_ring[1][half:, 512:], 1),
    ]
    qkv_pieces = relay_gather(qkv_plane, y_shift, mine[3:])
    theirs = [swap_cores(piece) for piece in mine]
    mlp_part = in_order(jnp.where(x == 0, mlp_own, mlp_moved), mine, qkv_pieces[1:3])
    mine, theirs, qkv_pieces = lax.optimization_barrier((mine, theirs, qkv_pieces))

    mlp_weights = lax.all_gather(mlp_part, ("dp", "z"), axis=0, tiled=False)
    mlp_order = jnp.stack(
        [(yy - y) % SIDE * SIDE + zz for zz in range(SIDE) for yy in range(SIDE)]
    ).astype(jnp.int32)

    token_count = SIDE * block_rows
    query_all, kv_own = call(
        qkv_kernel,
        (
            jax.ShapeDtypeStruct((token_count, 512), BF16),
            jax.ShapeDtypeStruct((token_count, 256), BF16),
        ),
        *mine,
        *theirs,
        *qkv_pieces,
        cos_all,
        sin_all,
        scalars=(block_ids * 128,),
        scratch=[
            pltpu.VMEM((token_count, width), BF16),
            pltpu.VMEM((width, 768), BF16),
        ],
        cost=(2 * token_count * width * 768, 10 << 20, 0),
        name="qkv",
    )
    out_far = z_shift(in_order(token_parts[3], query_all), 2)
    kv_pieces = relay_gather(kv_own, y_shift)

    qkv_pieces = in_order(qkv_pieces, kv_pieces[1])
    info_mine = jnp.concatenate(
        [
            piece[start + rows : start + rows + 1, : 2 * rows]
            for piece, start in plane_blocks(qkv_pieces, rows + 16)
        ],
        axis=0,
    )
    info_theirs = swap_cores(info_mine)
    info_mine, info_theirs = info_mine.astype(F32), info_theirs.astype(F32)
    seg_all = jnp.concatenate([info_mine[:, :rows], info_theirs[:, :rows]], axis=1)
    mod_all = jnp.concatenate([info_mine[:, rows:], info_theirs[:, rows:]], axis=1)
    pos_all = block_pos.astype(F32)
    key_info = jnp.concatenate([seg_all, jnp.where(mod_all == 1, seg_all, -2.0), pos_all], axis=0)
    query_info = jnp.stack(
        [
            seg_all[:SIDE].reshape(-1),
            jnp.where(mod_all == 1, seg_all, -1.0)[:SIDE].reshape(-1),
            pos_all[:SIDE].reshape(-1),
        ],
        axis=1,
    )
    first, last = jnp.min(seg_all, axis=1), jnp.max(seg_all, axis=1)
    q_first, q_last, q_id = first[:SIDE, None], last[:SIDE, None], block_ids[:SIDE, None]
    touches = (first[None, :] <= q_last) & (last[None, :] >= q_first)
    one_doc = (first == last)[None, :] & (q_first == q_last) & (first[None, :] == q_first)
    plain = one_doc & (block_ids[None, :] < q_id)
    kinds = jnp.where(plain, 1, jnp.where(touches, 2, 0)).astype(jnp.int32).reshape(-1)

    group = HEADS // KV_HEADS

    info_block = pl.BlockSpec((block_rows, 3), lambda i: (i, 0))
    head_block = pl.BlockSpec((block_rows, 512), lambda i: (i, 0))
    attended = pl.pallas_call(
        functools.partial(attend_kernel, block_rows),
        out_shape=jax.ShapeDtypeStruct((token_count, 512), BF16),
        grid=(SIDE,),
        in_specs=[SMEM, head_block, info_block, whole_block(key_info)]
        + [whole_block(piece) for piece in kv_pieces],
        out_specs=head_block,
        scratch_shapes=[
            pltpu.VMEM((16, block_rows, 256), BF16),
            pltpu.VMEM((16, group, block_rows, 256), F32),
            pltpu.VMEM((group, block_rows, HEAD_DIM), F32),
            pltpu.VMEM((group, block_rows, HEAD_DIM), F32),
            pltpu.VMEM((group, block_rows, HEAD_DIM), F32),
        ],
        compiler_params=pltpu.CompilerParams(vmem_limit_bytes=48 << 20),
        cost_estimate=pl.CostEstimate(
            flops=16 << 30, bytes_accessed=6 << 20, transcendentals=8 << 20
        ),
        name="attend",
    )(kinds, query_all, query_info, key_info, *kv_pieces)

    out_plane = jnp.concatenate([part[:, :512] for part in token_ring + [out_far]], axis=0)
    out_pieces = ring_gather(in_order(out_plane, kv_pieces), y_shift)
    table = call(
        table_kernel,
        jax.ShapeDtypeStruct((512, width), BF16),
        *out_pieces,
        scalars=(block_ids * 128,),
        cost=(1, 4 << 20, 0),
        name="table",
    )
    half_block = jax.ShapeDtypeStruct((rows, width), BF16)

    sums, arrived = [], []
    for place, z_place in enumerate((3, 1, 2, 0)):
        given = attended if place < 2 else in_order(attended, sums[place - 2])
        own, other = call(
            project_kernel,
            (half_block, half_block),
            given,
            table,
            specs=[
                pl.BlockSpec((block_rows, 512), lambda i, z_place=z_place: (z_place, 0)),
                whole_block(table),
            ],
            cost=(2 * block_rows * 512 * width, 4 << 20, 0),
            name="project",
        )
        both = own.astype(F32) + swap_cores(other).astype(F32)
        if z_place:
            both = both.astype(BF16)
            arrived.append(z_shift(both, STEPS[z_place]))
            sums.append(both)
    total = hidden_in.astype(F32) + both
    for part in arrived:
        total = total + part.astype(F32)
    residual = total.astype(BF16)

    normed_two = rms_normed(residual, mlp_gain)
    def weight_block(first):
        return pl.BlockSpec((16, 128, 128), lambda i: (0, first + i, 0))

    chunk = rows
    chunk_count = 2 * SIDE * chunk
    out_half = jax.ShapeDtypeStruct((chunk_count // 2, width // 2), BF16)

    def lift(mine, theirs):
        return pl.pallas_call(
            lift_kernel,
            out_shape=jax.ShapeDtypeStruct((blocks, chunk_count, 128), BF16),
            grid=(blocks,),
            in_specs=[SMEM]
            + [whole_block(piece) for piece in mine + theirs]
            + [weight_block(0), weight_block(blocks)],
            out_specs=pl.BlockSpec((1, chunk_count, 128), lambda i: (i, 0, 0)),
            scratch_shapes=[pltpu.VMEM((chunk_count, width), BF16)],
            compiler_params=pltpu.CompilerParams(vmem_limit_bytes=48 << 20),
            cost_estimate=pl.CostEstimate(
                flops=4 * chunk_count * width * hidden_units,
                bytes_accessed=10 << 20,
                transcendentals=chunk_count * hidden_units,
            ),
            name="lift",
        )(mlp_order, *mine, *theirs, mlp_weights, mlp_weights)

    def lower(inner, first):
        def down_block(side):
            return pl.BlockSpec(
                (1, hidden_units, 128), lambda i, order: (order[first + 2 * i + side], 2, 0)
            )

        out_block = pl.BlockSpec((chunk_count // 2, 256), lambda i, order: (0, i))
        return pl.pallas_call(
            lower_kernel,
            out_shape=(out_half, out_half),
            grid_spec=pltpu.PrefetchScalarGridSpec(
                num_scalar_prefetch=1,
                grid=(width // 512,),
                in_specs=[whole_block(inner), down_block(0), down_block(1)],
                out_specs=(out_block, out_block),
            ),
            compiler_params=pltpu.CompilerParams(vmem_limit_bytes=48 << 20),
            cost_estimate=pl.CostEstimate(
                flops=chunk_count * width * hidden_units,
                bytes_accessed=4 << 20,
                transcendentals=0,
            ),
            name="lower",
        )(mlp_order, inner, mlp_weights, mlp_weights)

    def spread(own, other):
        both = own.astype(F32) + swap_cores(other).astype(F32)
        parts = [
            y_shift(both[place * chunk : (place + 1) * chunk].astype(BF16), STEPS[place])
            for place in (3, 1, 2)
        ]
        return both[:chunk], parts

    mine = relay_gather(normed_two, y_shift)
    inner = lift(mine, [swap_cores(piece) for piece in mine])
    halves = []
    for start in (0, width // 2):
        kept, parts = spread(*lower(inner, start // 128))
        total = residual[:, start : start + width // 2].astype(F32) + kept
        for part in parts:
            total = total + part.astype(F32)
        halves.append(total.astype(BF16))
    return jnp.concatenate(halves, axis=1)


def solution(mesh):
    apart = jax.sharding.Mesh(
        mesh.devices.reshape(SIDE, SIDE, SIDE, 2), ("dp", "z", "y", "tensor")
    )
    seq = ("z", "y")
    tokens = P(("dp", "z", "y", "tensor"))
    inward, outward = P(seq, "tensor"), P("tensor", seq)
    placed = (
        tokens,
        P(),
        inward,
        inward,
        inward,
        outward,
        P(),
        inward,
        inward,
        outward,
        tokens,
        tokens,
    )
    return jax.shard_map(
        per_device, mesh=apart, in_specs=placed, out_specs=tokens, check_vma=False
    )
```

```python
import functools

import jax
import jax.numpy as jnp
from jax import lax
from jax.experimental import pallas as pl
from jax.experimental.pallas import tpu as pltpu
from jax.sharding import PartitionSpec as P

HEADS = 32
KV_HEADS = 8
HEAD_DIM = 128
EPSILON = 1e-05
THETA = 500000.0
SIDE = 4
BF16 = jnp.bfloat16
F32 = jnp.float32
SMEM = pl.BlockSpec(memory_space=pltpu.SMEM)
STEPS = (0, -1, 1, 2)


def x_shift(value, step):
    return lax.ppermute(value, "dp", [(i, (i + step) % SIDE) for i in range(SIDE)])


def y_shift(value, step):
    return lax.ppermute(value, "y", [(i, (i + step) % SIDE) for i in range(SIDE)])


def z_shift(value, step):
    return lax.ppermute(value, "z", [(i, (i + step) % SIDE) for i in range(SIDE)])


def plane_shift(value):
    return lax.ppermute(
        value,
        ("dp", "y"),
        [(x * SIDE + (y + x) % SIDE, x * SIDE + y) for x in range(1, SIDE) for y in range(SIDE)],
    )


def swap_cores(value):
    return lax.ppermute(value, "tensor", [(0, 1), (1, 0)])


def ring_gather(value, shift):
    return [value if step == 0 else shift(value, -step) for step in STEPS]


def relay_gather(value, shift, *earlier):
    half = value.shape[0] // 2
    before, after = shift(value, 1), shift(value, -1)
    low, high = in_order((after[:half], before[half:]), *earlier)
    return [value, before, after, shift(low, -1), shift(high, 1)]


def in_order(values, *earlier):
    kept = lax.optimization_barrier((values, earlier))
    return kept[0]


def place_tokens(mine, theirs, whole):
    rows, width = mine[0].shape[0], whole.shape[1]
    for which, pieces in enumerate((mine, theirs)):
        for place in range(SIDE):
            start = (2 * place + which) * rows
            for piece in pieces[place : None if place == 3 else place + 1]:
                whole[start : start + piece.shape[0], :] = piece[:, piece.shape[1] - width :]
                start += piece.shape[0]


def plane_blocks(pieces, rows):
    for piece in pieces:
        for start in range(0, piece.shape[0], rows):
            yield piece, start


def cut_kernel(places, query, key, value, segments, modes, out, gate, up, down, *refs):
    parts, packed = refs[:-1], refs[-1]
    rows = query.shape[0]
    for turn in range(SIDE):
        place, part = places[turn], parts[turn]
        wide, narrow = pl.multiple_of(place * 512, 512), pl.multiple_of(place * 128, 128)
        part[:rows, :512] = query[:, pl.ds(wide, 512)]
        part[:rows, 512:640] = key[:, pl.ds(narrow, 128)]
        part[:rows, 640:768] = value[:, pl.ds(narrow, 128)]
        below = part.shape[0] - rows
        for start, row in ((0, segments), (rows, modes)):
            part[rows:, start : start + rows] = jnp.broadcast_to(
                row[...].astype(F32), (below, rows)
            ).astype(BF16)
        part[rows:, 2 * rows :] = jnp.zeros((below, part.shape[1] - 2 * rows), BF16)
        if part.shape[1] > 768:
            for block in range(0, 512, 128):
                part[:rows, 768 + block : 896 + block] = out[
                    pl.ds(pl.multiple_of(place * 512 + block, 128), 128), :
                ]
    units = gate.shape[1]
    for block in range(units // 128):
        start = block * 128
        packed[start : start + 128, :] = gate[:, start : start + 128]
        packed[units + start : units + start + 128, :] = up[:, start : start + 128]
    packed[2 * units :, :] = down[...]


def norm_kernel(places, hidden, gain, out, *parts):
    normed = rms_normed(hidden[...], gain[...])
    for turn, part in enumerate(parts):
        place = places[turn]
        for block in range(0, 512, 128):
            part[:, block : block + 128] = out[
                pl.ds(pl.multiple_of(place * 512 + block, 128), 128), :
            ]
        part[:, 512:] = normed


def rms_normed(values, gain_vec):
    widened = values.astype(F32)
    mean_square = jnp.mean(widened * widened, axis=-1, keepdims=True)
    return (widened * lax.rsqrt(mean_square + EPSILON) * gain_vec).astype(BF16)


def qkv_kernel(offsets, *refs):
    mine, theirs, weights = refs[0:5], refs[5:10], refs[10:15]
    cosine, sine, query_out, kv_out, info_out, tokens, table = refs[15:]
    place_tokens(mine, theirs, tokens)
    depth = 128
    for slot, (source, start) in enumerate(plane_blocks(weights, weights[0].shape[0] // SIDE)):
        row = pl.multiple_of(offsets[slot], depth)
        table[pl.ds(row, depth), :] = source[start : start + depth, :]
        info = source[start + depth : start + depth + 16, :256].astype(F32)
        info_out[slot : slot + 1, :] = info[:1]
    cos_all, sin_all = cosine[...], sine[...]

    def rotated(part):
        return part * cos_all + pltpu.roll(part, HEAD_DIM // 2, 1) * sin_all

    for block in range(3):
        sums = jnp.dot(
            tokens[...], table[:, block * 256 : block * 256 + 256], preferred_element_type=F32
        )
        first, second = sums[:, :HEAD_DIM], sums[:, HEAD_DIM:]
        if block < 2:
            query_out[:, block * 256 : block * 256 + HEAD_DIM] = rotated(first).astype(BF16)
            query_out[:, block * 256 + HEAD_DIM : block * 256 + 256] = rotated(second).astype(BF16)
        else:
            kv_out[:, :HEAD_DIM] = rotated(first).astype(BF16)
            kv_out[:, HEAD_DIM:] = second.astype(BF16)


def attend_kernel(block_rows, kinds, query, query_info, key_info, *refs):
    kv_pieces = refs[0:5]
    out, kv_all, scores, top, total, mixed = refs[5:]
    z_place = pl.program_id(0)
    group = HEADS // KV_HEADS
    scale = HEAD_DIM**-0.5 * 1.4426950408889634

    @pl.when(z_place == 0)
    def _():
        for slot, (source, start) in enumerate(plane_blocks(kv_pieces, block_rows)):
            kv_all[slot] = source[start : start + block_rows, :]

    top[...] = jnp.full(top.shape, -1e30, F32)
    total[...] = jnp.zeros_like(total)
    mixed[...] = jnp.zeros_like(mixed)

    def score_of(head, key):
        return lax.dot_general(
            query[:, head * HEAD_DIM : (head + 1) * HEAD_DIM],
            key,
            (((1,), (1,)), ((), ())),
            preferred_element_type=F32,
        )

    def keep(slot, head, score):
        scores[slot, head] = score
        top[head] = jnp.maximum(
            top[head], jnp.maximum(score[:, :HEAD_DIM], score[:, HEAD_DIM:])
        )

    def first_pass(slot, carry):
        kind = kinds[z_place * 16 + slot]

        @pl.when(kind == 1)
        def _():
            key = kv_all[slot, :, :HEAD_DIM]
            for head in range(group):
                keep(slot, head, score_of(head, key))

        @pl.when(kind == 2)
        def _():
            key = kv_all[slot, :, :HEAD_DIM]
            key_seg = key_info[pl.ds(slot, 1), :]
            key_video = key_info[pl.ds(16 + slot, 1), :]
            key_pos = key_info[pl.ds(32 + slot, 1), :]
            same = query_info[:, 0:1] == key_seg
            video = query_info[:, 1:2] == key_video
            earlier = key_pos <= query_info[:, 2:3]
            allowed = video | (same & earlier)
            for head in range(group):
                keep(slot, head, jnp.where(allowed, score_of(head, key), -1e30))

        return carry

    lax.fori_loop(0, 16, first_pass, 0)
    for head in range(group):
        top[head] = jnp.broadcast_to(
            jnp.max(top[head], axis=-1, keepdims=True), top.shape[1:]
        )

    def second_pass(slot, carry):
        @pl.when(kinds[z_place * 16 + slot] > 0)
        def _():
            value = kv_all[slot, :, HEAD_DIM:]
            for head in range(group):
                high = top[head]
                left = jnp.exp2((scores[slot, head, :, :HEAD_DIM] - high) * scale)
                right = jnp.exp2((scores[slot, head, :, HEAD_DIM:] - high) * scale)
                total[head] = total[head] + (left + right)
                terms = jnp.concatenate([left.astype(BF16), right.astype(BF16)], axis=1)
                mixed[head] = mixed[head] + jnp.dot(terms, value, preferred_element_type=F32)

        return carry

    lax.fori_loop(0, 16, second_pass, 0)
    for head in range(group):
        out[:, head * HEAD_DIM : (head + 1) * HEAD_DIM] = (
            mixed[head] / jnp.sum(total[head], axis=-1, keepdims=True)
        ).astype(BF16)


def table_kernel(offsets, *refs):
    pieces, table = refs[:-1], refs[-1]
    for slot, (source, start) in enumerate(plane_blocks(pieces, 128)):
        column = pl.multiple_of(offsets[slot], 128)
        for block in range(0, 512, 128):
            table[block : block + 128, pl.ds(column, 128)] = source[
                start : start + 128, block : block + 128
            ]


def project_kernel(attended, table, own_out, other_out):
    half = own_out.shape[0]
    for start in range(0, table.shape[1], 512):
        part = jnp.dot(
            attended[...], table[:, start : start + 512], preferred_element_type=F32
        ).astype(BF16)
        own_out[:, start : start + 512] = part[:half]
        other_out[:, start : start + 512] = part[half:]


def lift_kernel(order, *refs):
    mine, theirs = refs[0:5], refs[5:10]
    gate, up, inner, tokens = refs[10:]

    @pl.when(pl.program_id(0) == 0)
    def _():
        place_tokens(mine, theirs, tokens)

    pair = jnp.concatenate(
        [
            jnp.concatenate([gate[order[block]], up[order[block]]], axis=1)
            for block in range(16)
        ],
        axis=0,
    )
    sums = jnp.dot(tokens[...], pair, preferred_element_type=F32)
    gated, lifted = sums[:, :128], sums[:, 128:]
    inner[0] = (gated / (1.0 + jnp.exp(-gated)) * lifted).astype(BF16)


def lower_kernel(order, inner, down_left, down_right, own_out, other_out):
    blocks, rows = inner.shape[0], inner.shape[1]
    lhs = jnp.concatenate([inner[block] for block in range(blocks)], axis=1)
    rhs = jnp.concatenate([down_left[0], down_right[0]], axis=1)
    part = jnp.dot(lhs, rhs, preferred_element_type=F32).astype(BF16)
    part = part.reshape(SIDE, 2, rows // 8, 256)
    own_out[...] = part[:, 0].reshape(rows // 2, 256)
    other_out[...] = part[:, 1].reshape(rows // 2, 256)


def whole_block(array):
    return pl.BlockSpec(array.shape, lambda *step: (0,) * array.ndim)


def call(kernel, out_shape, *operands, scalars=(), specs=None, scratch=(), cost=(1, 1, 0), name):
    specs = [whole_block(array) for array in operands] if specs is None else specs
    return pl.pallas_call(
        kernel,
        out_shape=out_shape,
        grid=(1,),
        in_specs=[SMEM] * len(scalars) + specs,
        out_specs=jax.tree.map(whole_block, out_shape),
        scratch_shapes=list(scratch),
        compiler_params=pltpu.CompilerParams(vmem_limit_bytes=48 << 20),
        cost_estimate=pl.CostEstimate(
            flops=cost[0], bytes_accessed=cost[1], transcendentals=cost[2]
        ),
        name=name,
    )(*scalars, *operands)


def per_device(
    hidden_in,
    attn_gain,
    query_weight,
    key_weight,
    value_weight,
    out_weight,
    mlp_gain,
    gate_weight,
    up_weight,
    down_weight,
    segment_ids,
    modality,
):
    x, z, y = lax.axis_index("dp"), lax.axis_index("z"), lax.axis_index("y")
    core = lax.axis_index("tensor")
    rows, width = hidden_in.shape
    block_rows = 2 * rows
    z_places = [(z + step) % SIDE for step in STEPS]
    y_places = [(y + step) % SIDE for step in STEPS]
    block_ids = jnp.stack([zz * SIDE + yy for yy in y_places for zz in z_places]).astype(jnp.int32)
    hidden_units = gate_weight.shape[1] // SIDE
    blocks = hidden_units // 128
    places = jnp.stack([(z - step) % SIDE for step in STEPS] + [(y - x) % SIDE]).astype(jnp.int32)

    def cut(kernel, shapes, whole, units, name):
        outs = [jax.ShapeDtypeStruct(shape, BF16) for shape in shapes]
        quarters = [
            pl.BlockSpec((128, hidden_units), lambda i, place: (0, place[SIDE])),
            pl.BlockSpec((128, hidden_units), lambda i, place: (0, place[SIDE])),
            pl.BlockSpec((hidden_units, 128), lambda i, place: (place[SIDE], 0)),
        ]
        return pl.pallas_call(
            kernel,
            out_shape=outs,
            grid_spec=pltpu.PrefetchScalarGridSpec(
                num_scalar_prefetch=1,
                grid=(1,),
                in_specs=[whole_block(array) for array in whole] + quarters[: len(units)],
                out_specs=[whole_block(out) for out in outs],
            ),
            compiler_params=pltpu.CompilerParams(vmem_limit_bytes=58 << 20),
            cost_estimate=pl.CostEstimate(flops=1, bytes_accessed=4 << 20, transcendentals=0),
            name=name,
        )(places, *whole, *units)

    def from_ring(parts):
        return [part if step == 0 else z_shift(part, -step) for part, step in zip(parts, STEPS)]

    in_block = (jnp.arange(block_rows, dtype=jnp.int32) + core * rows) % block_rows
    block_pos = block_ids[:, None] * block_rows + in_block[None, :]
    half_dim = HEAD_DIM // 2
    inverse_freq = THETA ** (-2.0 * jnp.arange(half_dim, dtype=F32) / HEAD_DIM)
    angles = block_pos[:SIDE].reshape(-1).astype(F32)[:, None] * inverse_freq[None, :]
    cosine, sine = jnp.cos(angles), jnp.sin(angles)
    cos_all = jnp.concatenate([cosine, cosine], axis=1)
    sin_all = jnp.concatenate([-sine, sine], axis=1)

    *qkv_parts, mlp_own = cut(
        cut_kernel,
        [(rows + 16, 768)] * 3 + [(rows + 16, 768 + 512), (3 * hidden_units, 128)],
        [
            query_weight,
            key_weight,
            value_weight,
            segment_ids.reshape(1, rows),
            modality.reshape(1, rows),
            out_weight,
        ],
        [gate_weight, up_weight, down_weight],
        "cut",
    )
    qkv_ring = from_ring(qkv_parts)
    mlp_moved = plane_shift(mlp_own)
    qkv_plane = jnp.concatenate([part[:, :768] for part in qkv_ring], axis=0)

    hidden, _ = lax.optimization_barrier((hidden_in, qkv_parts))
    token_parts = cut(
        norm_kernel,
        [(rows, 512 + width)] * 3,
        [hidden, attn_gain.reshape(1, width), out_weight],
        [],
        "norm",
    )
    token_ring = from_ring(token_parts)
    qkv_plane = in_order(qkv_plane, mlp_moved, token_parts, cos_all, sin_all)
    half = rows // 2
    mine = token_ring[:3] + [
        z_shift(token_ring[2][:half, 512:], -1),
        z_shift(token_ring[1][half:, 512:], 1),
    ]
    qkv_pieces = relay_gather(qkv_plane, y_shift, mine[3:])
    theirs = [swap_cores(piece) for piece in mine]
    mlp_part = in_order(jnp.where(x == 0, mlp_own, mlp_moved), mine, qkv_pieces[1:3])
    mine, theirs, qkv_pieces = lax.optimization_barrier((mine, theirs, qkv_pieces))

    mlp_weights = lax.all_gather(mlp_part, ("dp", "z"), axis=0, tiled=False)
    mlp_order = jnp.stack(
        [(yy - y) % SIDE * SIDE + zz for zz in range(SIDE) for yy in range(SIDE)]
    ).astype(jnp.int32)

    token_count = SIDE * block_rows
    query_all, kv_own, info_mine = call(
        qkv_kernel,
        (
            jax.ShapeDtypeStruct((token_count, 512), BF16),
            jax.ShapeDtypeStruct((token_count, 256), BF16),
            jax.ShapeDtypeStruct((SIDE * SIDE, 256), F32),
        ),
        *mine,
        *theirs,
        *qkv_pieces,
        cos_all,
        sin_all,
        scalars=(block_ids * 128,),
        scratch=[
            pltpu.VMEM((token_count, width), BF16),
            pltpu.VMEM((width, 768), BF16),
        ],
        cost=(2 * token_count * width * 768, 10 << 20, 0),
        name="qkv",
    )
    kv_pieces = relay_gather(kv_own, y_shift)

    info_theirs = swap_cores(info_mine)
    seg_all = jnp.concatenate([info_mine[:, :rows], info_theirs[:, :rows]], axis=1)
    mod_all = jnp.concatenate([info_mine[:, rows:], info_theirs[:, rows:]], axis=1)
    pos_all = block_pos.astype(F32)
    key_info = jnp.concatenate([seg_all, jnp.where(mod_all == 1, seg_all, -2.0), pos_all], axis=0)
    query_info = jnp.stack(
        [
            seg_all[:SIDE].reshape(-1),
            jnp.where(mod_all == 1, seg_all, -1.0)[:SIDE].reshape(-1),
            pos_all[:SIDE].reshape(-1),
        ],
        axis=1,
    )
    first, last = jnp.min(seg_all, axis=1), jnp.max(seg_all, axis=1)
    q_first, q_last, q_id = first[:SIDE, None], last[:SIDE, None], block_ids[:SIDE, None]
    touches = (first[None, :] <= q_last) & (last[None, :] >= q_first)
    one_doc = (first == last)[None, :] & (q_first == q_last) & (first[None, :] == q_first)
    plain = one_doc & (block_ids[None, :] < q_id)
    kinds = jnp.where(plain, 1, jnp.where(touches, 2, 0)).astype(jnp.int32).reshape(-1)

    group = HEADS // KV_HEADS

    info_block = pl.BlockSpec((block_rows, 3), lambda i: (i, 0))
    head_block = pl.BlockSpec((block_rows, 512), lambda i: (i, 0))
    attended = pl.pallas_call(
        functools.partial(attend_kernel, block_rows),
        out_shape=jax.ShapeDtypeStruct((token_count, 512), BF16),
        grid=(SIDE,),
        in_specs=[SMEM, head_block, info_block, whole_block(key_info)]
        + [whole_block(piece) for piece in kv_pieces],
        out_specs=head_block,
        scratch_shapes=[
            pltpu.VMEM((16, block_rows, 256), BF16),
            pltpu.VMEM((16, group, block_rows, 256), F32),
            pltpu.VMEM((group, block_rows, HEAD_DIM), F32),
            pltpu.VMEM((group, block_rows, HEAD_DIM), F32),
            pltpu.VMEM((group, block_rows, HEAD_DIM), F32),
        ],
        compiler_params=pltpu.CompilerParams(vmem_limit_bytes=48 << 20),
        cost_estimate=pl.CostEstimate(
            flops=16 << 30, bytes_accessed=6 << 20, transcendentals=8 << 20
        ),
        name="attend",
    )(kinds, query_all, query_info, key_info, *kv_pieces)

    out_plane = jnp.concatenate([part[:, :512] for part in token_ring] + [qkv_ring[3][:rows, 768:]], axis=0)
    out_pieces = ring_gather(in_order(out_plane, kv_pieces), y_shift)
    table = call(
        table_kernel,
        jax.ShapeDtypeStruct((512, width), BF16),
        *out_pieces,
        scalars=(block_ids * 128,),
        cost=(1, 4 << 20, 0),
        name="table",
    )
    half_block = jax.ShapeDtypeStruct((rows, width), BF16)

    sums, arrived = [], []
    for place, z_place in enumerate((3, 1, 2, 0)):
        given = attended if place < 2 else in_order(attended, sums[place - 2])
        own, other = call(
            project_kernel,
            (half_block, half_block),
            given,
            table,
            specs=[
                pl.BlockSpec((block_rows, 512), lambda i, z_place=z_place: (z_place, 0)),
                whole_block(table),
            ],
            cost=(2 * block_rows * 512 * width, 4 << 20, 0),
            name="project",
        )
        both = own.astype(F32) + swap_cores(other).astype(F32)
        if z_place:
            both = both.astype(BF16)
            arrived.append(z_shift(both, STEPS[z_place]))
            sums.append(both)
    total = hidden_in.astype(F32) + both
    for part in arrived:
        total = total + part.astype(F32)
    residual = total.astype(BF16)

    normed_two = rms_normed(residual, mlp_gain)
    def weight_block(first):
        return pl.BlockSpec((16, 128, 128), lambda i: (0, first + i, 0))

    chunk = rows
    chunk_count = 2 * SIDE * chunk
    out_half = jax.ShapeDtypeStruct((chunk_count // 2, width // 2), BF16)

    def lift(mine, theirs):
        return pl.pallas_call(
            lift_kernel,
            out_shape=jax.ShapeDtypeStruct((blocks, chunk_count, 128), BF16),
            grid=(blocks,),
            in_specs=[SMEM]
            + [whole_block(piece) for piece in mine + theirs]
            + [weight_block(0), weight_block(blocks)],
            out_specs=pl.BlockSpec((1, chunk_count, 128), lambda i: (i, 0, 0)),
            scratch_shapes=[pltpu.VMEM((chunk_count, width), BF16)],
            compiler_params=pltpu.CompilerParams(vmem_limit_bytes=48 << 20),
            cost_estimate=pl.CostEstimate(
                flops=4 * chunk_count * width * hidden_units,
                bytes_accessed=10 << 20,
                transcendentals=chunk_count * hidden_units,
            ),
            name="lift",
        )(mlp_order, *mine, *theirs, mlp_weights, mlp_weights)

    def lower(inner, first):
        def down_block(side):
            return pl.BlockSpec(
                (1, hidden_units, 128), lambda i, order: (order[first + 2 * i + side], 2, 0)
            )

        out_block = pl.BlockSpec((chunk_count // 2, 256), lambda i, order: (0, i))
        return pl.pallas_call(
            lower_kernel,
            out_shape=(out_half, out_half),
            grid_spec=pltpu.PrefetchScalarGridSpec(
                num_scalar_prefetch=1,
                grid=(width // 512,),
                in_specs=[whole_block(inner), down_block(0), down_block(1)],
                out_specs=(out_block, out_block),
            ),
            compiler_params=pltpu.CompilerParams(vmem_limit_bytes=48 << 20),
            cost_estimate=pl.CostEstimate(
                flops=chunk_count * width * hidden_units,
                bytes_accessed=4 << 20,
                transcendentals=0,
            ),
            name="lower",
        )(mlp_order, inner, mlp_weights, mlp_weights)

    def spread(own, other):
        both = own.astype(F32) + swap_cores(other).astype(F32)
        return both[:chunk], [
            both[place * chunk : (place + 1) * chunk].astype(BF16) for place in (3, 1, 2)
        ]

    mine = relay_gather(normed_two, y_shift)
    inner = lift(mine, [swap_cores(piece) for piece in mine])
    halves = []
    for start in (0, width // 2):
        kept, parts = spread(*lower(inner, start // 128))
        total = residual[:, start : start + width // 2].astype(F32) + kept
        for place, part in zip((3, 1, 2), parts):
            total = total + y_shift(part, STEPS[place]).astype(F32)
        halves.append(total.astype(BF16))
    return jnp.concatenate(halves, axis=1)


def solution(mesh):
    apart = jax.sharding.Mesh(
        mesh.devices.reshape(SIDE, SIDE, SIDE, 2), ("dp", "z", "y", "tensor")
    )
    seq = ("z", "y")
    tokens = P(("dp", "z", "y", "tensor"))
    inward, outward = P(seq, "tensor"), P("tensor", seq)
    placed = (
        tokens,
        P(),
        inward,
        inward,
        inward,
        outward,
        P(),
        inward,
        inward,
        outward,
        tokens,
        tokens,
    )
    return jax.shard_map(
        per_device, mesh=apart, in_specs=placed, out_specs=tokens, check_vma=False
    )
```

```python
import functools

import jax
import jax.numpy as jnp
from jax import lax
from jax.experimental import pallas as pl
from jax.experimental.pallas import tpu as pltpu
from jax.sharding import PartitionSpec as P

HEADS = 32
KV_HEADS = 8
HEAD_DIM = 128
EPSILON = 1e-05
THETA = 500000.0
SIDE = 4
BF16 = jnp.bfloat16
F32 = jnp.float32
SMEM = pl.BlockSpec(memory_space=pltpu.SMEM)
STEPS = (0, -1, 1, 2)


def x_shift(value, step):
    return lax.ppermute(value, "dp", [(i, (i + step) % SIDE) for i in range(SIDE)])


def y_shift(value, step):
    return lax.ppermute(value, "y", [(i, (i + step) % SIDE) for i in range(SIDE)])


def z_shift(value, step):
    return lax.ppermute(value, "z", [(i, (i + step) % SIDE) for i in range(SIDE)])


def plane_shift(value):
    return lax.ppermute(
        value,
        ("dp", "y"),
        [(x * SIDE + (y + x) % SIDE, x * SIDE + y) for x in range(1, SIDE) for y in range(SIDE)],
    )


def swap_cores(value):
    return lax.ppermute(value, "tensor", [(0, 1), (1, 0)])


def ring_gather(value, shift):
    return [value if step == 0 else shift(value, -step) for step in STEPS]


def relay_gather(value, shift, *earlier):
    half = value.shape[0] // 2
    before, after = shift(value, 1), shift(value, -1)
    low, high = in_order((after[:half], before[half:]), *earlier)
    return [value, before, after, shift(low, -1), shift(high, 1)]


def in_order(values, *earlier):
    kept = lax.optimization_barrier((values, earlier))
    return kept[0]


def place_tokens(mine, theirs, whole):
    rows, width = mine[0].shape[0], whole.shape[1]
    for which, pieces in enumerate((mine, theirs)):
        for place in range(SIDE):
            start = (2 * place + which) * rows
            for piece in pieces[place : None if place == 3 else place + 1]:
                whole[start : start + piece.shape[0], :] = piece[:, piece.shape[1] - width :]
                start += piece.shape[0]


def plane_blocks(pieces, rows):
    for piece in pieces:
        for start in range(0, piece.shape[0], rows):
            yield piece, start


def cut_kernel(places, query, key, value, segments, modes, out, gate, up, down, *refs):
    parts, packed = refs[:-1], refs[-1]
    rows = query.shape[0]
    for turn in range(SIDE):
        place, part = places[turn], parts[turn]
        wide, narrow = pl.multiple_of(place * 512, 512), pl.multiple_of(place * 128, 128)
        part[:rows, :512] = query[:, pl.ds(wide, 512)]
        part[:rows, 512:640] = key[:, pl.ds(narrow, 128)]
        part[:rows, 640:768] = value[:, pl.ds(narrow, 128)]
        below = part.shape[0] - rows
        for start, row in ((0, segments), (rows, modes)):
            part[rows:, start : start + rows] = jnp.broadcast_to(
                row[...].astype(F32), (below, rows)
            ).astype(BF16)
        part[rows:, 2 * rows :] = jnp.zeros((below, part.shape[1] - 2 * rows), BF16)
        if part.shape[1] > 768:
            for block in range(0, 512, 128):
                part[:rows, 768 + block : 896 + block] = out[
                    pl.ds(pl.multiple_of(place * 512 + block, 128), 128), :
                ]
    units = gate.shape[1]
    for block in range(units // 128):
        start = block * 128
        packed[start : start + 128, :] = gate[:, start : start + 128]
        packed[units + start : units + start + 128, :] = up[:, start : start + 128]
    packed[2 * units :, :] = down[...]


def norm_kernel(places, hidden, gain, out, *parts):
    normed = rms_normed(hidden[...], gain[...])
    for turn, part in enumerate(parts):
        place = places[turn]
        for block in range(0, 512, 128):
            part[:, block : block + 128] = out[
                pl.ds(pl.multiple_of(place * 512 + block, 128), 128), :
            ]
        part[:, 512:] = normed


def rms_normed(values, gain_vec):
    widened = values.astype(F32)
    mean_square = jnp.mean(widened * widened, axis=-1, keepdims=True)
    return (widened * lax.rsqrt(mean_square + EPSILON) * gain_vec).astype(BF16)


def qkv_kernel(offsets, *refs):
    mine, theirs, weights = refs[0:5], refs[5:10], refs[10:15]
    cosine, sine, query_out, kv_out, info_out, tokens, table = refs[15:]
    place_tokens(mine, theirs, tokens)
    depth = 128
    for slot, (source, start) in enumerate(plane_blocks(weights, weights[0].shape[0] // SIDE)):
        row = pl.multiple_of(offsets[slot], depth)
        table[pl.ds(row, depth), :] = source[start : start + depth, :]
        info = source[start + depth : start + depth + 16, :256].astype(F32)
        info_out[slot : slot + 1, :] = info[:1]
    cos_all, sin_all = cosine[...], sine[...]

    def rotated(part):
        return part * cos_all + pltpu.roll(part, HEAD_DIM // 2, 1) * sin_all

    for block in range(3):
        sums = jnp.dot(
            tokens[...], table[:, block * 256 : block * 256 + 256], preferred_element_type=F32
        )
        first, second = sums[:, :HEAD_DIM], sums[:, HEAD_DIM:]
        if block < 2:
            query_out[:, block * 256 : block * 256 + HEAD_DIM] = rotated(first).astype(BF16)
            query_out[:, block * 256 + HEAD_DIM : block * 256 + 256] = rotated(second).astype(BF16)
        else:
            kv_out[:, :HEAD_DIM] = rotated(first).astype(BF16)
            kv_out[:, HEAD_DIM:] = second.astype(BF16)


def attend_kernel(block_rows, kinds, query, query_info, key_info, *refs):
    kv_pieces = refs[0:5]
    out, kv_all, scores, top, total, mixed = refs[5:]
    z_place = pl.program_id(0)
    group = HEADS // KV_HEADS
    scale = HEAD_DIM**-0.5 * 1.4426950408889634

    @pl.when(z_place == 0)
    def _():
        for slot, (source, start) in enumerate(plane_blocks(kv_pieces, block_rows)):
            kv_all[slot] = source[start : start + block_rows, :]

    top[...] = jnp.full(top.shape, -1e30, F32)
    total[...] = jnp.zeros_like(total)
    mixed[...] = jnp.zeros_like(mixed)

    def score_of(head, key):
        return lax.dot_general(
            query[:, head * HEAD_DIM : (head + 1) * HEAD_DIM],
            key,
            (((1,), (1,)), ((), ())),
            preferred_element_type=F32,
        )

    def keep(slot, head, score):
        scores[slot, head] = score
        top[head] = jnp.maximum(
            top[head], jnp.maximum(score[:, :HEAD_DIM], score[:, HEAD_DIM:])
        )

    def first_pass(slot, carry):
        kind = kinds[z_place * 16 + slot]

        @pl.when(kind == 1)
        def _():
            key = kv_all[slot, :, :HEAD_DIM]
            for head in range(group):
                keep(slot, head, score_of(head, key))

        @pl.when(kind == 2)
        def _():
            key = kv_all[slot, :, :HEAD_DIM]
            key_seg = key_info[pl.ds(slot, 1), :]
            key_video = key_info[pl.ds(16 + slot, 1), :]
            key_pos = key_info[pl.ds(32 + slot, 1), :]
            same = query_info[:, 0:1] == key_seg
            video = query_info[:, 1:2] == key_video
            earlier = key_pos <= query_info[:, 2:3]
            allowed = video | (same & earlier)
            for head in range(group):
                keep(slot, head, jnp.where(allowed, score_of(head, key), -1e30))

        return carry

    lax.fori_loop(0, 16, first_pass, 0)
    for head in range(group):
        top[head] = jnp.broadcast_to(
            jnp.max(top[head], axis=-1, keepdims=True), top.shape[1:]
        )

    def second_pass(slot, carry):
        @pl.when(kinds[z_place * 16 + slot] > 0)
        def _():
            value = kv_all[slot, :, HEAD_DIM:]
            for head in range(group):
                high = top[head]
                left = jnp.exp2((scores[slot, head, :, :HEAD_DIM] - high) * scale)
                right = jnp.exp2((scores[slot, head, :, HEAD_DIM:] - high) * scale)
                total[head] = total[head] + (left + right)
                terms = jnp.concatenate([left.astype(BF16), right.astype(BF16)], axis=1)
                mixed[head] = mixed[head] + jnp.dot(terms, value, preferred_element_type=F32)

        return carry

    lax.fori_loop(0, 16, second_pass, 0)
    for head in range(group):
        out[:, head * HEAD_DIM : (head + 1) * HEAD_DIM] = (
            mixed[head] / jnp.sum(total[head], axis=-1, keepdims=True)
        ).astype(BF16)


def table_kernel(offsets, *refs):
    pieces, table = refs[:-1], refs[-1]
    for slot, (source, start) in enumerate(plane_blocks(pieces, 128)):
        column = pl.multiple_of(offsets[slot], 128)
        for block in range(0, 512, 128):
            table[block : block + 128, pl.ds(column, 128)] = source[
                start : start + 128, block : block + 128
            ]


def project_kernel(attended, table, own_out, other_out):
    half = own_out.shape[0]
    for start in range(0, table.shape[1], 512):
        part = jnp.dot(
            attended[...], table[:, start : start + 512], preferred_element_type=F32
        ).astype(BF16)
        own_out[:, start : start + 512] = part[:half]
        other_out[:, start : start + 512] = part[half:]


def lift_kernel(order, *refs):
    mine, theirs = refs[0:5], refs[5:10]
    gate, up, inner, tokens = refs[10:]

    @pl.when(pl.program_id(0) == 0)
    def _():
        place_tokens(mine, theirs, tokens)

    pair = jnp.concatenate(
        [
            jnp.concatenate([gate[order[block]], up[order[block]]], axis=1)
            for block in range(16)
        ],
        axis=0,
    )
    sums = jnp.dot(tokens[...], pair, preferred_element_type=F32)
    gated, lifted = sums[:, :128], sums[:, 128:]
    inner[0] = (gated / (1.0 + jnp.exp(-gated)) * lifted).astype(BF16)


def lower_kernel(order, inner, down_left, down_right, own_out, other_out):
    blocks, rows = inner.shape[0], inner.shape[1]
    lhs = jnp.concatenate([inner[block] for block in range(blocks)], axis=1)
    rhs = jnp.concatenate([down_left[0], down_right[0]], axis=1)
    part = jnp.dot(lhs, rhs, preferred_element_type=F32).astype(BF16)
    part = part.reshape(SIDE, 2, rows // 8, 256)
    own_out[...] = part[:, 0].reshape(rows // 2, 256)
    other_out[...] = part[:, 1].reshape(rows // 2, 256)


def whole_block(array):
    return pl.BlockSpec(array.shape, lambda *step: (0,) * array.ndim)


def call(kernel, out_shape, *operands, scalars=(), specs=None, scratch=(), cost=(1, 1, 0), name):
    specs = [whole_block(array) for array in operands] if specs is None else specs
    return pl.pallas_call(
        kernel,
        out_shape=out_shape,
        grid=(1,),
        in_specs=[SMEM] * len(scalars) + specs,
        out_specs=jax.tree.map(whole_block, out_shape),
        scratch_shapes=list(scratch),
        compiler_params=pltpu.CompilerParams(vmem_limit_bytes=48 << 20),
        cost_estimate=pl.CostEstimate(
            flops=cost[0], bytes_accessed=cost[1], transcendentals=cost[2]
        ),
        name=name,
    )(*scalars, *operands)


def per_device(
    hidden_in,
    attn_gain,
    query_weight,
    key_weight,
    value_weight,
    out_weight,
    mlp_gain,
    gate_weight,
    up_weight,
    down_weight,
    segment_ids,
    modality,
):
    x, z, y = lax.axis_index("dp"), lax.axis_index("z"), lax.axis_index("y")
    core = lax.axis_index("tensor")
    rows, width = hidden_in.shape
    block_rows = 2 * rows
    z_places = [(z + step) % SIDE for step in STEPS]
    y_places = [(y + step) % SIDE for step in STEPS]
    block_ids = jnp.stack([zz * SIDE + yy for yy in y_places for zz in z_places]).astype(jnp.int32)
    hidden_units = gate_weight.shape[1] // SIDE
    blocks = hidden_units // 128
    places = jnp.stack([(z - step) % SIDE for step in STEPS] + [(y - x) % SIDE]).astype(jnp.int32)

    def cut(kernel, shapes, whole, units, name):
        outs = [jax.ShapeDtypeStruct(shape, BF16) for shape in shapes]
        quarters = [
            pl.BlockSpec((128, hidden_units), lambda i, place: (0, place[SIDE])),
            pl.BlockSpec((128, hidden_units), lambda i, place: (0, place[SIDE])),
            pl.BlockSpec((hidden_units, 128), lambda i, place: (place[SIDE], 0)),
        ]
        return pl.pallas_call(
            kernel,
            out_shape=outs,
            grid_spec=pltpu.PrefetchScalarGridSpec(
                num_scalar_prefetch=1,
                grid=(1,),
                in_specs=[whole_block(array) for array in whole] + quarters[: len(units)],
                out_specs=[whole_block(out) for out in outs],
            ),
            compiler_params=pltpu.CompilerParams(vmem_limit_bytes=58 << 20),
            cost_estimate=pl.CostEstimate(flops=1, bytes_accessed=4 << 20, transcendentals=0),
            name=name,
        )(places, *whole, *units)

    def from_ring(parts):
        return [part if step == 0 else z_shift(part, -step) for part, step in zip(parts, STEPS)]

    in_block = (jnp.arange(block_rows, dtype=jnp.int32) + core * rows) % block_rows
    block_pos = block_ids[:, None] * block_rows + in_block[None, :]
    half_dim = HEAD_DIM // 2
    inverse_freq = THETA ** (-2.0 * jnp.arange(half_dim, dtype=F32) / HEAD_DIM)
    angles = block_pos[:SIDE].reshape(-1).astype(F32)[:, None] * inverse_freq[None, :]
    cosine, sine = jnp.cos(angles), jnp.sin(angles)
    cos_all = jnp.concatenate([cosine, cosine], axis=1)
    sin_all = jnp.concatenate([-sine, sine], axis=1)

    *qkv_parts, mlp_own = cut(
        cut_kernel,
        [(rows + 16, 768)] * 3 + [(rows + 16, 768 + 512), (3 * hidden_units, 128)],
        [
            query_weight,
            key_weight,
            value_weight,
            segment_ids.reshape(1, rows),
            modality.reshape(1, rows),
            out_weight,
        ],
        [gate_weight, up_weight, down_weight],
        "cut",
    )
    qkv_ring = from_ring(qkv_parts)
    mlp_moved = plane_shift(mlp_own)
    qkv_plane = jnp.concatenate([part[:, :768] for part in qkv_ring], axis=0)

    hidden, _ = lax.optimization_barrier((hidden_in, qkv_parts))
    token_parts = cut(
        norm_kernel,
        [(rows, 512 + width)] * 3,
        [hidden, attn_gain.reshape(1, width), out_weight],
        [],
        "norm",
    )
    token_ring = from_ring(token_parts)
    qkv_plane = in_order(qkv_plane, mlp_moved, token_parts)
    half = rows // 2
    low, high = in_order(
        (token_ring[2][:half, 512:], token_ring[1][half:, 512:]), cos_all, sin_all
    )
    mine = token_ring[:3] + [z_shift(low, -1), z_shift(high, 1)]
    qkv_pieces = relay_gather(qkv_plane, y_shift, mine[3:])
    theirs = [swap_cores(piece) for piece in mine]
    mlp_part = in_order(jnp.where(x == 0, mlp_own, mlp_moved), mine, qkv_pieces[1:3])
    mine, theirs, qkv_pieces = lax.optimization_barrier((mine, theirs, qkv_pieces))

    mlp_weights = lax.all_gather(mlp_part, ("dp", "z"), axis=0, tiled=False)
    mlp_order = jnp.stack(
        [(yy - y) % SIDE * SIDE + zz for zz in range(SIDE) for yy in range(SIDE)]
    ).astype(jnp.int32)

    token_count = SIDE * block_rows
    query_all, kv_own, info_mine = call(
        qkv_kernel,
        (
            jax.ShapeDtypeStruct((token_count, 512), BF16),
            jax.ShapeDtypeStruct((token_count, 256), BF16),
            jax.ShapeDtypeStruct((SIDE * SIDE, 256), F32),
        ),
        *mine,
        *theirs,
        *qkv_pieces,
        cos_all,
        sin_all,
        scalars=(block_ids * 128,),
        scratch=[
            pltpu.VMEM((token_count, width), BF16),
            pltpu.VMEM((width, 768), BF16),
        ],
        cost=(2 * token_count * width * 768, 10 << 20, 0),
        name="qkv",
    )
    kv_pieces = relay_gather(kv_own, y_shift)

    info_theirs = swap_cores(info_mine)
    seg_all = jnp.concatenate([info_mine[:, :rows], info_theirs[:, :rows]], axis=1)
    mod_all = jnp.concatenate([info_mine[:, rows:], info_theirs[:, rows:]], axis=1)
    pos_all = block_pos.astype(F32)
    key_info = jnp.concatenate([seg_all, jnp.where(mod_all == 1, seg_all, -2.0), pos_all], axis=0)
    query_info = jnp.stack(
        [
            seg_all[:SIDE].reshape(-1),
            jnp.where(mod_all == 1, seg_all, -1.0)[:SIDE].reshape(-1),
            pos_all[:SIDE].reshape(-1),
        ],
        axis=1,
    )
    first, last = jnp.min(seg_all, axis=1), jnp.max(seg_all, axis=1)
    q_first, q_last, q_id = first[:SIDE, None], last[:SIDE, None], block_ids[:SIDE, None]
    touches = (first[None, :] <= q_last) & (last[None, :] >= q_first)
    one_doc = (first == last)[None, :] & (q_first == q_last) & (first[None, :] == q_first)
    plain = one_doc & (block_ids[None, :] < q_id)
    kinds = jnp.where(plain, 1, jnp.where(touches, 2, 0)).astype(jnp.int32).reshape(-1)

    group = HEADS // KV_HEADS

    info_block = pl.BlockSpec((block_rows, 3), lambda i: (i, 0))
    head_block = pl.BlockSpec((block_rows, 512), lambda i: (i, 0))
    attended = pl.pallas_call(
        functools.partial(attend_kernel, block_rows),
        out_shape=jax.ShapeDtypeStruct((token_count, 512), BF16),
        grid=(SIDE,),
        in_specs=[SMEM, head_block, info_block, whole_block(key_info)]
        + [whole_block(piece) for piece in kv_pieces],
        out_specs=head_block,
        scratch_shapes=[
            pltpu.VMEM((16, block_rows, 256), BF16),
            pltpu.VMEM((16, group, block_rows, 256), F32),
            pltpu.VMEM((group, block_rows, HEAD_DIM), F32),
            pltpu.VMEM((group, block_rows, HEAD_DIM), F32),
            pltpu.VMEM((group, block_rows, HEAD_DIM), F32),
        ],
        compiler_params=pltpu.CompilerParams(vmem_limit_bytes=48 << 20),
        cost_estimate=pl.CostEstimate(
            flops=16 << 30, bytes_accessed=6 << 20, transcendentals=8 << 20
        ),
        name="attend",
    )(kinds, query_all, query_info, key_info, *kv_pieces)

    out_plane = jnp.concatenate([part[:, :512] for part in token_ring] + [qkv_ring[3][:rows, 768:]], axis=0)
    out_pieces = ring_gather(in_order(out_plane, kv_pieces), y_shift)
    table = call(
        table_kernel,
        jax.ShapeDtypeStruct((512, width), BF16),
        *out_pieces,
        scalars=(block_ids * 128,),
        cost=(1, 4 << 20, 0),
        name="table",
    )
    half_block = jax.ShapeDtypeStruct((rows, width), BF16)

    sums, arrived = [], []
    for place, z_place in enumerate((3, 1, 2, 0)):
        given = attended if place < 2 else in_order(attended, sums[place - 2])
        own, other = call(
            project_kernel,
            (half_block, half_block),
            given,
            table,
            specs=[
                pl.BlockSpec((block_rows, 512), lambda i, z_place=z_place: (z_place, 0)),
                whole_block(table),
            ],
            cost=(2 * block_rows * 512 * width, 4 << 20, 0),
            name="project",
        )
        both = own.astype(F32) + swap_cores(other).astype(F32)
        if z_place:
            both = both.astype(BF16)
            arrived.append(z_shift(both, STEPS[z_place]))
            sums.append(both)
    total = hidden_in.astype(F32) + both
    for part in arrived:
        total = total + part.astype(F32)
    residual = total.astype(BF16)

    normed_two = rms_normed(residual, mlp_gain)
    def weight_block(first):
        return pl.BlockSpec((16, 128, 128), lambda i: (0, first + i, 0))

    chunk = rows
    chunk_count = 2 * SIDE * chunk
    out_half = jax.ShapeDtypeStruct((chunk_count // 2, width // 2), BF16)

    def lift(mine, theirs):
        return pl.pallas_call(
            lift_kernel,
            out_shape=jax.ShapeDtypeStruct((blocks, chunk_count, 128), BF16),
            grid=(blocks,),
            in_specs=[SMEM]
            + [whole_block(piece) for piece in mine + theirs]
            + [weight_block(0), weight_block(blocks)],
            out_specs=pl.BlockSpec((1, chunk_count, 128), lambda i: (i, 0, 0)),
            scratch_shapes=[pltpu.VMEM((chunk_count, width), BF16)],
            compiler_params=pltpu.CompilerParams(vmem_limit_bytes=48 << 20),
            cost_estimate=pl.CostEstimate(
                flops=4 * chunk_count * width * hidden_units,
                bytes_accessed=10 << 20,
                transcendentals=chunk_count * hidden_units,
            ),
            name="lift",
        )(mlp_order, *mine, *theirs, mlp_weights, mlp_weights)

    def lower(inner, first):
        def down_block(side):
            return pl.BlockSpec(
                (1, hidden_units, 128), lambda i, order: (order[first + 2 * i + side], 2, 0)
            )

        out_block = pl.BlockSpec((chunk_count // 2, 256), lambda i, order: (0, i))
        return pl.pallas_call(
            lower_kernel,
            out_shape=(out_half, out_half),
            grid_spec=pltpu.PrefetchScalarGridSpec(
                num_scalar_prefetch=1,
                grid=(width // 512,),
                in_specs=[whole_block(inner), down_block(0), down_block(1)],
                out_specs=(out_block, out_block),
            ),
            compiler_params=pltpu.CompilerParams(vmem_limit_bytes=48 << 20),
            cost_estimate=pl.CostEstimate(
                flops=chunk_count * width * hidden_units,
                bytes_accessed=4 << 20,
                transcendentals=0,
            ),
            name="lower",
        )(mlp_order, inner, mlp_weights, mlp_weights)

    def spread(own, other):
        both = own.astype(F32) + swap_cores(other).astype(F32)
        return both[:chunk], [
            both[place * chunk : (place + 1) * chunk].astype(BF16) for place in (3, 1, 2)
        ]

    mine = relay_gather(normed_two, y_shift)
    inner = lift(mine, [swap_cores(piece) for piece in mine])
    halves = []
    for start in (0, width // 2):
        kept, parts = spread(*lower(inner, start // 128))
        total = residual[:, start : start + width // 2].astype(F32) + kept
        for place, part in zip((3, 1, 2), parts):
            total = total + y_shift(part, STEPS[place]).astype(F32)
        halves.append(total.astype(BF16))
    return jnp.concatenate(halves, axis=1)


def solution(mesh):
    apart = jax.sharding.Mesh(
        mesh.devices.reshape(SIDE, SIDE, SIDE, 2), ("dp", "z", "y", "tensor")
    )
    seq = ("z", "y")
    tokens = P(("dp", "z", "y", "tensor"))
    inward, outward = P(seq, "tensor"), P("tensor", seq)
    placed = (
        tokens,
        P(),
        inward,
        inward,
        inward,
        outward,
        P(),
        inward,
        inward,
        outward,
        tokens,
        tokens,
    )
    return jax.shard_map(
        per_device, mesh=apart, in_specs=placed, out_specs=tokens, check_vma=False
    )
```
